128 devices in a mesh: blk: 16 (over y_lo, z, core), col: 8 (over y_hi, x).
Axes of the slice: x: 4, y: 4 (y_hi: 2, y_lo: 2; y = y_hi * 2 + y_lo), z: 4, core: 2. Of those that a mesh axis runs over, the one named last changes fastest.
Arguments:
- features: bfloat16 [384, 256, 256], P('blk', 'col'), may hold values from -6 to 6
- cotangent: bfloat16 [384, 256, 256], P('blk', 'col'), may hold values from -6 to 6
- w_self: bfloat16 [256, 256], replicated, may hold values from -0.375 to 0.375
- w_neigh: bfloat16 [256, 256], replicated, may hold values from -0.375 to 0.375
- tile_row: int32 [2048], P('blk'), may hold values from 0 to 23
- tile_owner: int32 [2048, 1], P('blk'), may hold values from 0 to 15; in each aligned block of 128 rows (0 to 127, 128 to 255, ...) at most 12 rows name the same one
- tile_col: int32 [2048], P('blk'), may hold values from 0 to 23
- tile_count: int32 [16], P('blk'), may hold values from 96 to 128, as said below
- edge_dst: int32 [2048, 640], P('blk'), may hold values from 0 to 255
- edge_src: int32 [2048, 640], P('blk'), may hold values from 0 to 255
Outputs:
- hidden: bfloat16 [384, 256, 256], P('blk', 'col')
- input_grad: bfloat16 [384, 256, 256], P('blk', 'col')
- self_grad: float32 [256, 256], P('col')
- neigh_grad: float32 [256, 256], P('col')
The draws below stay inside these ranges and needn't reach their ends.
Inputs may be any that keep to these rules, and one draw needn't show every extreme that they name: `tile_owner`: among the 128 slots of one index of blk, no owner is named more than 12 times. `tile_count`: every index of blk keeps all 128 or three quarters of its slots live, always the first ones; some index keeps all.
All inputs are finite; a program needn't handle non-finite values.
Results may differ from the reference program's by a relative error of at most 0.007.
Values may be sent and summed in bfloat16 or wider, within the bound.
No kernel may reach another device: no remote copies, remote signals or barrier semaphores. Data moves between devices by JAX's collectives and lax.ppermute only.
A program may use at most 128 MiB of HBM per device.

```python
import math
import jax
import jax.numpy as jnp
import numpy as np
from jax import lax

F = 256
TILE = 256
BPD = 24
TILES_DEV = 128
EDGES = 640
MOST = 12
NBT = 384
TILES = 2048
N_BLK = 16


def draw_tile_count(key, part):
    key = jax.random.fold_in(key, 11)
    picks = jax.random.randint(jax.random.fold_in(key, 1), (N_BLK,), 0, 2)
    counts = jnp.where(picks == 0, TILES_DEV, 3 * TILES_DEV // 4)
    full_index = jax.random.randint(jax.random.fold_in(key, 2), (), 0, N_BLK)
    return jnp.where(jnp.arange(N_BLK) == full_index, TILES_DEV, counts).astype(jnp.int32)


def touch_ends(drawn, own_key, least, top_value):
    longest = drawn.shape.index(max(drawn.shape))
    spots = []
    for shift in (0, 1):
        where = [jax.random.randint(jax.random.fold_in(own_key, axis), (), 0, length) for axis, length in enumerate(drawn.shape)]
        where[longest] = (where[longest] + shift) % drawn.shape[longest]
        spots.append(tuple(where))
    return drawn.at[spots[0]].set(least).at[spots[1]].set(top_value)


def levels(own_key, extent, shards, smallest, high):
    def one(axis_at, parts):
        draws = jax.random.uniform(jax.random.fold_in(jax.random.fold_in(own_key, 6), axis_at), (parts,), jnp.float32, smallest / len(shards), high / len(shards))
        return jnp.repeat(jnp.exp(draws), extent[axis_at] // parts).reshape((-1,) + (1,) * (len(extent) - axis_at - 1))

    gain = one(*shards[0])
    for cut in shards[1:]:
        gain = gain * one(*cut)
    return gain


def deal_out(stream_key, own, number, rows, amount, top, most, lean):
    order = jax.random.permutation(stream_key, amount)
    heavy_load, ordinary = shares(amount, rows * top, most, lean, True), shares(amount, rows * top, most, lean, False)
    places = jnp.arange(amount)

    def named(lengths, turn):
        used = int((lengths > 0).sum())
        fixed = max(1, used // 4)
        passed = fixed + (places - fixed + turn * (used - fixed)) % max(1, amount - fixed)
        return jnp.zeros((amount,), jnp.int32).at[order[jnp.where(places < fixed, places, passed)]].set(jnp.asarray(lengths, jnp.int32))

    lengths = jnp.where(number % 4 == 0, named(heavy_load, number // 4), named(ordinary, number - number // 4 - 1))
    mixed = jax.random.permutation(jax.random.fold_in(own, 3), amount)
    giver, sink = mixed[0:amount // 2 * 2:2], mixed[1:amount // 2 * 2:2]
    room = jnp.minimum(lengths[giver] - 1, most - lengths[sink]) // 2
    room = jnp.where((giver == order[0]) | (sink == order[0]) | (lengths[sink] == 0), 0, jnp.maximum(room, 0))
    passed = jax.random.randint(jax.random.fold_in(own, 4), (amount // 2,), 0, 1 << 20) % (room + 1)
    lengths = lengths.at[giver].add(-passed).at[sink].add(passed)
    items = jnp.searchsorted(jnp.cumsum(lengths), jnp.arange(rows * top), side="right").astype(jnp.int32)
    grid = items.reshape(top, rows).T
    grid = grid[jax.random.permutation(jax.random.fold_in(own, 1), rows)]
    turn = jax.random.randint(jax.random.fold_in(own, 2), (rows, 1), 0, top)
    return jnp.take_along_axis(grid, (jnp.arange(top)[None, :] + turn) % top, axis=1)


def shares(amount, total, most, lean, full):
    loads = [(1 << 20) // math.isqrt(rank ** lean) + 1 for rank in range(1, amount + 1)]
    largest = most if full else min(most, max(-(-total // amount), total * loads[0] // sum(loads)))
    least = 1 if total - largest >= amount - 1 else 0
    holding, surplus = [largest] + [least] * (amount - 1), total - largest - least * (amount - 1)
    while surplus > 0:
        movable = [i for i in range(1, amount) if holding[i] < largest] or [i for i in range(1, amount) if holding[i] < most]
        pool, remaining = sum([loads[i] for i in movable]), surplus
        for i in movable:
            addition = min(most - holding[i], max(1, remaining * loads[i] // pool), surplus)
            holding[i] = holding[i] + addition
            surplus = surplus - addition
    return np.array(holding)


def normal_values(own_key, dims, width, most, cuts=(), kind=jnp.bfloat16):
    entries = width * jax.random.normal(own_key, dims, jnp.float32)
    if cuts:
        entries = entries * levels(own_key, dims, cuts, -0.22, 0.18)
    return jnp.clip(entries, -most, most).astype(kind)


def setup_inputs(seed: int = 0) -> dict:
    key_of = jax.random.split(jax.random.key(seed), 11)
    features = normal_values(key_of[0], (NBT, F, TILE), 1.0, 6.0, ((0, 16), (1, 8)))
    cotangent = normal_values(key_of[1], (NBT, F, TILE), 1.0, 6.0, ((0, 16), (1, 8)))
    w_self = normal_values(key_of[2], (F, F), F ** -0.5, 0.375)
    w_neigh = normal_values(key_of[3], (F, F), F ** -0.5, 0.375)
    tile_row = touch_ends(jax.random.randint(key_of[4], (TILES,), 0, BPD), jax.random.fold_in(key_of[4], 1), 0, BPD - 1).astype(jnp.int32)
    tile_owner_keys = jax.random.split(jax.random.fold_in(key_of[5], 1), TILES // TILES_DEV)
    tile_owner_turns = jax.random.permutation(jax.random.fold_in(key_of[5], 3), TILES // TILES_DEV)
    tile_owner = jax.vmap(lambda own, number: deal_out(jax.random.fold_in(key_of[5], 2), own, number, TILES_DEV, N_BLK, 1, MOST, 2))(tile_owner_keys, tile_owner_turns).reshape((TILES, 1))
    tile_col = touch_ends(jax.random.randint(key_of[6], (TILES,), 0, BPD), jax.random.fold_in(key_of[6], 1), 0, BPD - 1).astype(jnp.int32)
    tile_count = draw_tile_count(jax.random.fold_in(key_of[10], 71), 0)
    edge_dst = touch_ends(jax.random.randint(key_of[8], (TILES, EDGES), 0, TILE), jax.random.fold_in(key_of[8], 1), 0, TILE - 1).astype(jnp.int32)
    edge_src = touch_ends(jax.random.randint(key_of[9], (TILES, EDGES), 0, TILE), jax.random.fold_in(key_of[9], 1), 0, TILE - 1).astype(jnp.int32)
    return {"features": features, "cotangent": cotangent, "w_self": w_self, "w_neigh": w_neigh, "tile_row": tile_row, "tile_owner": tile_owner, "tile_col": tile_col, "tile_count": tile_count, "edge_dst": edge_dst, "edge_src": edge_src}


def reference(features, cotangent, w_self, w_neigh, tile_row, tile_owner, tile_col, tile_count, edge_dst, edge_src):
    tile_blocks = features.shape[0]
    node_count = tile_blocks * TILE
    node_feats = jnp.transpose(features, (0, 2, 1)).reshape(node_count, F)
    cot_nodes = jnp.transpose(cotangent, (0, 2, 1)).reshape(node_count, F).astype(jnp.float32)
    slot_ids = jnp.arange(N_BLK * TILES_DEV, dtype=jnp.int32)
    holder = slot_ids // TILES_DEV
    tile_live = (slot_ids % TILES_DEV < tile_count[holder]).astype(jnp.float32)
    dst_tile = (holder * BPD + tile_row).astype(jnp.int32)
    src_tile = (tile_owner[:, 0] * BPD + tile_col).astype(jnp.int32)
    dst_node = (dst_tile[:, None] * TILE + edge_dst).reshape(N_BLK, -1).astype(jnp.int32)
    src_node = (src_tile[:, None] * TILE + edge_src).reshape(N_BLK, -1).astype(jnp.int32)
    edge_live = jnp.broadcast_to(tile_live[:, None], edge_dst.shape).reshape(N_BLK, -1)

    def forward_step(running, edge_item):
        feat_sums, degree = running
        dst_ids, src_ids, weights = edge_item
        rows = node_feats[src_ids].astype(jnp.float32) * weights[:, None]
        feat_sums = feat_sums + jax.ops.segment_sum(rows, dst_ids, num_segments=node_count)
        degree = degree + jax.ops.segment_sum(weights, dst_ids, num_segments=node_count)
        return ((feat_sums, degree), None)
    start_sums = (jnp.zeros((node_count, F), jnp.float32), jnp.zeros((node_count,), jnp.float32))
    (feat_sums, degree), _ = lax.scan(forward_step, start_sums, (dst_node, src_node, edge_live))
    inverse = 1.0 / jnp.maximum(degree, 1.0)
    mean = (feat_sums * inverse[:, None]).astype(jnp.bfloat16)
    preact = jnp.dot(node_feats, w_self, preferred_element_type=jnp.float32) + jnp.dot(mean, w_neigh, preferred_element_type=jnp.float32)
    gate_value = jax.nn.sigmoid(preact)
    hidden = (preact * gate_value).astype(jnp.bfloat16)
    out_grad = (cot_nodes * gate_value * (1.0 + preact * (1.0 - gate_value))).astype(jnp.bfloat16)
    self_term = jnp.dot(out_grad, w_self.T, preferred_element_type=jnp.float32)
    pre_grad = (jnp.dot(out_grad, w_neigh.T, preferred_element_type=jnp.float32) * inverse[:, None]).astype(jnp.bfloat16)

    def backward_step(back_sums, slot_item):
        dst_t, src_t, live_now, dst_ids, src_ids = slot_item
        rows = pre_grad[dst_t * TILE + dst_ids].astype(jnp.float32) * live_now
        partial_value = jax.ops.segment_sum(rows, src_ids, num_segments=TILE).astype(jnp.bfloat16)
        partial_value = lax.optimization_barrier(partial_value).astype(jnp.float32)
        start = (src_t * TILE).astype(jnp.int32)
        block = lax.dynamic_slice_in_dim(back_sums, start, TILE, 0)
        return (lax.dynamic_update_slice_in_dim(back_sums, block + partial_value, start, 0), None)
    back_sums, _ = lax.scan(backward_step, jnp.zeros((node_count, F), jnp.float32), (dst_tile, src_tile, tile_live, edge_dst, edge_src))
    input_grad = (self_term + back_sums).astype(jnp.bfloat16)
    grad_scale = 1.0 / math.sqrt(node_count)
    self_grad = jnp.dot(node_feats.T, out_grad, preferred_element_type=jnp.float32) * grad_scale
    neigh_grad = jnp.dot(mean.T, out_grad, preferred_element_type=jnp.float32) * grad_scale
    hidden_out = jnp.transpose(hidden.reshape(tile_blocks, TILE, F), (0, 2, 1))
    grad_out = jnp.transpose(input_grad.reshape(tile_blocks, TILE, F), (0, 2, 1))
    return (hidden_out, grad_out, self_grad, neigh_grad)
```

```python
import functools
import math

import jax
import jax.numpy as jnp
from jax import lax
from jax.experimental import pallas as pl
from jax.experimental.pallas import tpu as pltpu
from jax.sharding import PartitionSpec as P

GROUP = 8
VMEM_BYTES = 48 * 1024 * 1024


def adjacency_kernel(row_ref, count_ref, src_ref, dst_ref, adj_ref, inv_ref, deg_ref):
    step = pl.program_id(0)
    width = adj_ref.shape[1]
    edges = src_ref.shape[1]

    @pl.when(step == 0)
    def _():
        deg_ref[...] = jnp.zeros_like(deg_ref)

    lane_index = lax.broadcasted_iota(jnp.int32, (width, edges), 0)
    for j in range(GROUP):
        slot = step * GROUP + j
        alive = slot < count_ref[0]
        src = src_ref[j : j + 1, :]
        dst = jnp.where(alive, dst_ref[j : j + 1, :], -1)
        spread = jnp.where(lane_index == src, 1.0, 0.0).astype(jnp.bfloat16)
        collect = jnp.where(lane_index == dst, 1.0, 0.0).astype(jnp.bfloat16)
        adj = lax.dot_general(
            spread, collect, (((1,), (1,)), ((), ())), preferred_element_type=jnp.float32
        )
        adj_ref[j] = adj.astype(jnp.bfloat16)
        row = row_ref[slot]
        deg_ref[row] += jnp.sum(adj.reshape(width // 8, 8, width), axis=0)

    @pl.when(step == pl.num_programs(0) - 1)
    def _():
        degree = jnp.sum(deg_ref[...], axis=1, keepdims=True)
        inv_ref[...] = 1.0 / jnp.maximum(degree, 1.0)


def build_adjacency(tile_row, tile_count, edge_src, edge_dst, blocks, width):
    slots, edges = edge_src.shape
    return pl.pallas_call(
        adjacency_kernel,
        grid_spec=pltpu.PrefetchScalarGridSpec(
            num_scalar_prefetch=2,
            grid=(slots // GROUP,),
            in_specs=[
                pl.BlockSpec((GROUP, edges), lambda i, *_: (i, 0)),
                pl.BlockSpec((GROUP, edges), lambda i, *_: (i, 0)),
            ],
            out_specs=[
                pl.BlockSpec((GROUP, width, width), lambda i, *_: (i, 0, 0)),
                pl.BlockSpec((blocks, 1, width), lambda i, *_: (0, 0, 0)),
            ],
            scratch_shapes=[pltpu.VMEM((blocks, 8, width), jnp.float32)],
        ),
        out_shape=[
            jax.ShapeDtypeStruct((slots, width, width), jnp.bfloat16),
            jax.ShapeDtypeStruct((blocks, 1, width), jnp.float32),
        ],
        compiler_params=pltpu.CompilerParams(vmem_limit_bytes=VMEM_BYTES),
        cost_estimate=pl.CostEstimate(
            flops=2 * slots * edges * width * width,
            bytes_accessed=slots * width * width * 2,
            transcendentals=0,
        ),
        name="adjacency",
    )(tile_row, tile_count, edge_src, edge_dst)


def mean_kernel(row_ref, source_ref, feats_ref, adj_ref, inv_ref, mean_ref, sum_ref):
    step = pl.program_id(0)

    @pl.when(step == 0)
    def _():
        sum_ref[...] = jnp.zeros_like(sum_ref)

    for j in range(GROUP):
        slot = step * GROUP + j
        flow = jnp.dot(
            feats_ref[source_ref[slot]], adj_ref[j], preferred_element_type=jnp.float32
        )
        sum_ref[row_ref[slot]] += flow

    @pl.when(step == pl.num_programs(0) - 1)
    def _():
        mean_ref[...] = (sum_ref[...] * inv_ref[...]).astype(jnp.bfloat16)


def neighbor_mean(tile_row, source, feats, adj, inverse):
    slots, width, _ = adj.shape
    nodes, cols, _ = feats.shape
    blocks = inverse.shape[0]
    whole = pl.BlockSpec(memory_space=pltpu.VMEM)
    return pl.pallas_call(
        mean_kernel,
        grid_spec=pltpu.PrefetchScalarGridSpec(
            num_scalar_prefetch=2,
            grid=(slots // GROUP,),
            in_specs=[
                whole,
                pl.BlockSpec((GROUP, width, width), lambda i, *_: (i, 0, 0)),
                whole,
            ],
            out_specs=whole,
            scratch_shapes=[pltpu.VMEM((blocks, cols, width), jnp.float32)],
        ),
        out_shape=jax.ShapeDtypeStruct((blocks, cols, width), jnp.bfloat16),
        compiler_params=pltpu.CompilerParams(vmem_limit_bytes=VMEM_BYTES),
        name="neighbor_mean",
    )(tile_row, source, feats, adj, inverse)


def dense_kernel(
    x_ref, mean_ref, cot_ref, ws_ref, wn_ref, wst_ref, wnt_ref, inv_ref,
    hidden_ref, self_ref, pre_ref, gs_ref, gn_ref,
):
    step = pl.program_id(0)
    parts, _, cols, width = x_ref.shape
    feats = parts * cols
    x = x_ref[...].reshape(feats, width)
    mean = mean_ref[...].reshape(feats, width)
    cot = cot_ref[...].reshape(feats, width).astype(jnp.float32)
    preact = jnp.dot(wst_ref[...], x, preferred_element_type=jnp.float32)
    preact = preact + jnp.dot(wnt_ref[...], mean, preferred_element_type=jnp.float32)
    gate = jax.nn.sigmoid(preact)
    hidden_ref[...] = (preact * gate).astype(jnp.bfloat16).reshape(parts, 1, cols, width)
    out_grad = (cot * gate * (1.0 + preact * (1.0 - gate))).astype(jnp.bfloat16)
    self_term = jnp.dot(ws_ref[...], out_grad, preferred_element_type=jnp.float32)
    self_ref[...] = self_term.astype(self_ref.dtype).reshape(parts, 1, cols, width)
    pre = jnp.dot(wn_ref[...], out_grad, preferred_element_type=jnp.float32) * inv_ref[0]
    pre_ref[...] = pre.astype(jnp.bfloat16).reshape(parts, 1, cols, width)

    @pl.when(step == 0)
    def _():
        gs_ref[...] = jnp.zeros_like(gs_ref)
        gn_ref[...] = jnp.zeros_like(gn_ref)

    nt = (((1,), (1,)), ((), ()))
    gs_ref[...] += lax.dot_general(x, out_grad, nt, preferred_element_type=jnp.float32)
    gn_ref[...] += lax.dot_general(mean, out_grad, nt, preferred_element_type=jnp.float32)


def dense(x, mean, cot, w_self, w_neigh, inverse):
    parts, rows, cols, width = x.shape
    feats = parts * cols
    part = pl.BlockSpec((parts, 1, cols, width), lambda i: (0, i, 0, 0))
    weight = pl.BlockSpec((feats, feats), lambda i: (0, 0))
    moved = jax.ShapeDtypeStruct(x.shape, jnp.bfloat16)
    grad = jax.ShapeDtypeStruct((feats, feats), jnp.float32)
    return pl.pallas_call(
        dense_kernel,
        grid=(rows,),
        in_specs=[part, part, part, weight, weight, weight, weight,
                  pl.BlockSpec((1, 1, width), lambda i: (i, 0, 0))],
        out_specs=[part, part, part, weight, weight],
        out_shape=[moved, moved, moved, grad, grad],
        compiler_params=pltpu.CompilerParams(vmem_limit_bytes=VMEM_BYTES),
        name="dense",
    )(x, mean, cot, w_self, w_neigh, w_self.T, w_neigh.T, inverse)


def back_kernel(row_ref, source_ref, grads_ref, adj_ref, out_ref, sum_ref):
    step = pl.program_id(0)

    @pl.when(step == 0)
    def _():
        sum_ref[...] = jnp.zeros_like(sum_ref)

    for j in range(GROUP):
        slot = step * GROUP + j
        back = lax.dot_general(
            grads_ref[row_ref[slot]], adj_ref[j], (((1,), (1,)), ((), ())),
            preferred_element_type=jnp.float32,
        )
        sum_ref[source_ref[slot]] += back.astype(jnp.bfloat16).astype(jnp.float32)

    @pl.when(step == pl.num_programs(0) - 1)
    def _():
        out_ref[...] = sum_ref[...].astype(jnp.bfloat16)


def transposed_sums(tile_row, source, grads, adj, nodes):
    slots, width, _ = adj.shape
    _, cols, _ = grads.shape
    whole = pl.BlockSpec(memory_space=pltpu.VMEM)
    return pl.pallas_call(
        back_kernel,
        grid_spec=pltpu.PrefetchScalarGridSpec(
            num_scalar_prefetch=2,
            grid=(slots // GROUP,),
            in_specs=[whole, pl.BlockSpec((GROUP, width, width), lambda i, *_: (i, 0, 0))],
            out_specs=whole,
            scratch_shapes=[pltpu.VMEM((nodes, cols, width), jnp.float32)],
        ),
        out_shape=jax.ShapeDtypeStruct((nodes, cols, width), jnp.bfloat16),
        compiler_params=pltpu.CompilerParams(vmem_limit_bytes=VMEM_BYTES),
        name="transposed_sums",
    )(tile_row, source, grads, adj)


def local(
    features, cotangent, w_self, w_neigh, tile_row, tile_owner, tile_col, tile_count,
    edge_dst, edge_src,
):
    blocks, cols, width = features.shape
    n_blk, n_col = lax.axis_size("blk"), lax.axis_size("col")
    per = blocks // n_col
    source = tile_owner[:, 0] * blocks + tile_col

    def to_nodes(a):
        return lax.all_to_all(a.reshape(n_col, per, cols, width), "col", 0, 0)

    def to_feats(a):
        return lax.all_to_all(a, "col", 0, 0).reshape(blocks, cols, width)

    gathered = lax.all_gather(features, "blk", axis=0, tiled=True)
    adj, inverse = build_adjacency(tile_row, tile_count, edge_src, edge_dst, blocks, width)
    x_nodes, cot_nodes = to_nodes(features), to_nodes(cotangent)
    mean = neighbor_mean(tile_row, source, gathered, adj, inverse)
    mean_nodes = to_nodes(mean)
    own_inverse = lax.dynamic_slice_in_dim(inverse, lax.axis_index("col") * per, per, 0)
    hidden, self_term, pre_grad, self_part, neigh_part = dense(
        x_nodes, mean_nodes, cot_nodes, w_self, w_neigh, own_inverse
    )
    pre_feats = to_feats(pre_grad)
    back = transposed_sums(tile_row, source, pre_feats, adj, blocks * n_blk)
    returned = lax.psum_scatter(back, "blk", scatter_dimension=0, tiled=True)
    input_grad = (
        to_feats(self_term).astype(jnp.float32) + returned.astype(jnp.float32)
    ).astype(jnp.bfloat16)

    feats = n_col * cols
    parts = jnp.stack([self_part, neigh_part]).reshape(2, n_col, cols, feats)
    total = jnp.sum(lax.all_to_all(parts, "col", 1, 1), axis=1)
    for bit in range(n_blk.bit_length() - 1):
        total = total + lax.ppermute(
            total, "blk", [(i, i ^ (1 << bit)) for i in range(n_blk)]
        )
    total = total * (1.0 / math.sqrt(blocks * width * n_blk))
    return (to_feats(hidden), input_grad, total[0], total[1])


def solution(mesh):
    placed = (
        P("blk", "col", None),
        P("blk", "col", None),
        P(),
        P(),
        P("blk"),
        P("blk", None),
        P("blk"),
        P("blk"),
        P("blk", None),
        P("blk", None),
    )
    return jax.shard_map(
        local,
        mesh=mesh,
        in_specs=placed,
        out_specs=(P("blk", "col", None), P("blk", "col", None), P("col", None), P("col", None)),
        check_vma=False,
    )
```

```python
import functools
import math

import jax
import jax.numpy as jnp
from jax import lax
from jax.experimental import pallas as pl
from jax.experimental.pallas import tpu as pltpu
from jax.sharding import PartitionSpec as P

UNROLL = 8
HERE = 160
ROWS = 168
CUTS = (0, 8, 16)
VMEM_BYTES = 14 * 1024 * 1024
NT = (((1,), (1,)), ((), ()))
WHOLE = pl.BlockSpec(memory_space=pltpu.VMEM)
IDLE = pl.BlockSpec(memory_space=pl.ANY)
SCALARS = pl.BlockSpec(memory_space=pltpu.SMEM)

VIEW = (0, 2, 6, 1, 3, 4, 7, 5)


def turned(i, dz):
    y, z, core = i >> 3, (i >> 1) & 3, i & 1
    return (y << 3) | (((z + dz) % 4) << 1) | core


ROUTES = {
    "up": [(i, turned(i, 1)) for i in range(16)],
    "down": [(i, turned(i, -1)) for i in range(16)],
    "over": [(i, i ^ 8) for i in range(16)],
    "core": [(i, i ^ 1) for i in range(16)],
}


def send(value, route):
    return lax.ppermute(value, "blk", ROUTES[route])


def call(
    kernel, out_shape, operands, scalars=(), scratch=(), aliases=None, flops=0, name=None,
    idle=(), idle_out=0,
):
    out_specs = [WHOLE] * (len(out_shape) - idle_out) + [IDLE] * idle_out
    return pl.pallas_call(
        kernel,
        in_specs=[SCALARS] * len(scalars) + [WHOLE] * len(operands) + [IDLE] * len(idle),
        out_specs=out_specs,
        out_shape=out_shape,
        scratch_shapes=list(scratch),
        input_output_aliases=aliases or {},
        compiler_params=pltpu.CompilerParams(vmem_limit_bytes=VMEM_BYTES),
        cost_estimate=pl.CostEstimate(flops=flops, bytes_accessed=0, transcendentals=0),
        name=name,
    )(*scalars, *operands, *idle)


def one_hot(ids, lanes):
    hit = jnp.where(
        lanes == ids.astype(jnp.bfloat16), jnp.ones((), jnp.bfloat16), jnp.zeros((), jnp.bfloat16)
    )
    return hit.astype(jnp.float8_e4m3fn)


def adjacency_kernel(first, last, fresh, final, plan_ref, edge_ref, *refs):
    if fresh:
        weight_ref, refs = refs[0], refs[1:]
    else:
        refs = refs[2:]
    adj_ref, deg_ref, refs = refs[0], refs[1], refs[2:]
    width = adj_ref.shape[1]
    edges = edge_ref.shape[1]
    if fresh:
        deg_ref[...] = jnp.zeros_like(deg_ref)
        turn_ref = refs[0]
        for k in range(2):
            turn_ref[k] = weight_ref[k]
            turn_ref[2 + k] = weight_ref[k].T
    lanes = lax.broadcasted_iota(jnp.int32, (width, edges), 0).astype(jnp.bfloat16)

    def body(i, carry):
        base = pl.multiple_of(i * 8, 8)
        both = edge_ref[pl.ds(base, 8), :]
        src, dst = both & 255, both >> 8
        for j in range(8):
            spread, collect = one_hot(src[j : j + 1], lanes), one_hot(dst[j : j + 1], lanes)
            adj = lax.dot_general(spread, collect, NT, preferred_element_type=jnp.float32)
            adj_ref[base + j] = adj.astype(jnp.bfloat16)
            deg_ref[plan_ref[ROWS + base + j]] += jnp.sum(adj.reshape(width // 8, 8, width), axis=0)
        return carry

    lax.fori_loop(first, last, body, 0)
    if final:
        inv_ref = refs[0]
        blocks = inv_ref.shape[0]
        degree = jnp.sum(deg_ref[:blocks], axis=1, keepdims=True)
        inv_ref[...] = 1.0 / jnp.maximum(degree, 1.0)


def adjacency(k, plan, edges, blocks, width, weights=None, state=()):
    slots, count = edges.shape
    fresh, final = k == 0, k == len(CUTS) - 2
    outs = [
        jax.ShapeDtypeStruct((slots, width, width), jnp.bfloat16),
        jax.ShapeDtypeStruct((blocks + 1, 8, width), jnp.float32),
    ]
    if fresh:
        outs.append(jax.ShapeDtypeStruct((4,) + weights.shape[1:], jnp.bfloat16))
    if final:
        outs.append(jax.ShapeDtypeStruct((blocks, 1, width), jnp.float32))
    return call(
        functools.partial(adjacency_kernel, CUTS[k], CUTS[k + 1], fresh, final),
        outs,
        (edges, *((weights,) if fresh else state)),
        (plan,),
        aliases=None if fresh else {2: 0, 3: 1},
        flops=2 * 8 * (CUTS[k + 1] - CUTS[k]) * count * width * width,
        name="adjacency",
    )


def near_kernel(own_ref, less_ref, more_ref, over_ref, kept_ref, deg_ref, near_ref, one_ref, two_ref):
    rows = own_ref.shape[0]
    for k, ref in enumerate((own_ref, less_ref, more_ref, over_ref)):
        near_ref[k * rows : (k + 1) * rows] = ref[...]
    one_ref[...] = more_ref[...]
    two_ref[...] = over_ref[...]


def join_near(pieces, deg):
    rows, cols, width = pieces[0].shape
    return call(
        near_kernel,
        [jax.ShapeDtypeStruct(deg.shape, deg.dtype)]
        + [jax.ShapeDtypeStruct((n, cols, width), jnp.bfloat16) for n in (4 * rows, rows, rows)],
        (*pieces, deg),
        aliases={4: 0},
        name="join",
    )


def mid_kernel(more_ref, less_ref, two_ref, kept_ref, inv_ref, mid_ref, *outs):
    rows = more_ref.shape[0]
    third = rows // 3
    for k, ref in enumerate((more_ref, less_ref, two_ref)):
        mid_ref[k * rows : (k + 1) * rows] = ref[...]
    outs[0][...] = two_ref[:third]
    outs[1][...] = less_ref[third : 2 * third]
    outs[2][...] = more_ref[2 * third :]


def join_mid(pieces, inverse):
    rows, cols, width = pieces[0].shape
    sizes = (3 * rows,) + (rows // 3,) * 3
    return call(
        mid_kernel,
        [jax.ShapeDtypeStruct(inverse.shape, inverse.dtype)]
        + [jax.ShapeDtypeStruct((n, cols, width), jnp.bfloat16) for n in sizes],
        (*pieces, inverse),
        aliases={3: 0},
        name="join",
    )


def far_kernel(one_ref, two_ref, three_ref, kept_ref, sum_ref, far_ref):
    rows = one_ref.shape[0]
    for k, ref in enumerate((one_ref, two_ref, three_ref)):
        far_ref[k * rows : (k + 1) * rows] = ref[...]


def join_far(pieces, sums):
    rows, cols, width = pieces[0].shape
    return call(
        far_kernel,
        [
            jax.ShapeDtypeStruct(sums.shape, sums.dtype),
            jax.ShapeDtypeStruct((3 * rows, cols, width), jnp.bfloat16),
        ],
        (*pieces, sums),
        aliases={3: 0},
        name="join",
    )


def ranged(start, stop, body):
    def step(i, carry):
        for j in range(UNROLL):
            spot = start + i * UNROLL + j
            body(jnp.minimum(spot, stop - 1), spot < stop)
        return carry

    lax.fori_loop(0, (stop - start + UNROLL - 1) // UNROLL, step, 0)


def fields(item):
    return item & 127, (item >> 7) & 31, (item >> 12) & 31, (item >> 17) & 15, item >> 21


def mean_kernel(low, high, fresh, final, idle, plan_ref, adj_ref, here_ref, swap_ref, *refs):
    if not fresh:
        refs = refs[1:]
    if final:
        inv_ref, x_ref, cot_ref, refs = *refs[:3], refs[3:]
    refs = refs[idle:]
    sum_ref = refs[0]
    blocks = sum_ref.shape[0] - 1
    slots = adj_ref.shape[0]
    if fresh:
        sum_ref[...] = jnp.zeros_like(sum_ref)
    if final:
        out_ref = refs[1]
        parts, rows, cols, width = out_ref.shape
        rows = rows // 3
        out_ref[:, rows : 2 * rows] = x_ref[...].reshape(parts, rows, cols, width)
        out_ref[:, 2 * rows :] = cot_ref[...].reshape(parts, rows, cols, width)

    for core, feats_ref in enumerate((here_ref, swap_ref)):
        def add(spot, valid):
            slot, row, col, key, _ = fields(plan_ref[spot])
            place = (key - low - 8 * core) * blocks + col
            flow = jnp.dot(feats_ref[place], adj_ref[slot], preferred_element_type=jnp.float32)
            sum_ref[jnp.where(valid, row, blocks)] += flow

        ranged(plan_ref[slots + low + 8 * core], plan_ref[slots + high + 8 * core], add)
    if final:
        mean = (sum_ref[:blocks] * inv_ref[...]).astype(jnp.bfloat16)
        out_ref[:, :rows] = mean.reshape(parts, rows, cols, width)


def mean_stage(plan, adj, low, high, pieces, before=None, last=(), parts=0, idle=()):
    rows, cols, width = pieces[0].shape
    blocks = rows // (high - low)
    fresh, final = before is None, len(last) > 0
    outs = [jax.ShapeDtypeStruct((blocks + 1, cols, width), jnp.float32)]
    if final:
        outs.append(jax.ShapeDtypeStruct((parts, 3 * blocks // parts, cols, width), jnp.bfloat16))
    return call(
        functools.partial(mean_kernel, low, high, fresh, final, len(idle)),
        outs,
        [adj, *pieces] + ([] if fresh else [before]) + list(last),
        (plan,),
        aliases=None if fresh else {4: 0},
        flops=2 * (high - low) * 16 * width**3,
        idle=idle,
        name="neighbor_mean",
    )[-1]


def dense_kernel(plan_ref, in_ref, turn_ref, inv_ref, adj_ref, out_ref, kept_ref, gs_ref, gn_ref):
    parts, rows, cols, width = in_ref.shape
    rows = rows // 3
    feats = parts * cols
    here = plan_ref[HERE]
    for i in range(rows):
        mean = in_ref[:, i].reshape(feats, width)
        x = in_ref[:, rows + i].reshape(feats, width)
        cot = in_ref[:, 2 * rows + i].reshape(feats, width).astype(jnp.float32)
        preact = jnp.dot(turn_ref[2], x, preferred_element_type=jnp.float32)
        preact = preact + jnp.dot(turn_ref[3], mean, preferred_element_type=jnp.float32)
        gate = jax.nn.sigmoid(preact)
        hidden = (preact * gate).astype(jnp.bfloat16)
        out_ref[:, rows + i] = hidden.reshape(parts, cols, width)
        out_grad = (cot * gate * (1.0 + preact * (1.0 - gate))).astype(jnp.bfloat16)
        self_term = jnp.dot(turn_ref[0], out_grad, preferred_element_type=jnp.float32)
        out_ref[:, 2 * rows + i] = self_term.astype(jnp.bfloat16).reshape(parts, cols, width)
        pre = jnp.dot(turn_ref[1], out_grad, preferred_element_type=jnp.float32)
        pre = pre * inv_ref[here * rows + i]
        out_ref[:, i] = pre.astype(jnp.bfloat16).reshape(parts, cols, width)
        for ref, left in ((gs_ref, x), (gn_ref, mean)):
            term = lax.dot_general(left, out_grad, NT, preferred_element_type=jnp.float32)
            ref[...] = ref[...] + term if i else term
    for k, ref in enumerate((gs_ref, gn_ref)):
        out_ref[:, 3 * rows + k] = ref[...].astype(jnp.bfloat16).reshape(parts, cols, width)


def dense(plan, packed, turn, inverse, adj):
    parts, rows, cols, width = packed.shape
    feats = parts * cols
    grad = pltpu.VMEM((feats, feats), jnp.float32)
    return call(
        dense_kernel,
        [
            jax.ShapeDtypeStruct((parts, rows + 2, cols, width), jnp.bfloat16),
            jax.ShapeDtypeStruct(adj.shape, adj.dtype),
        ],
        (packed, turn, inverse, adj),
        (plan,),
        [grad, grad],
        aliases={4: 1},
        flops=4 * rows * width * feats * feats,
        name="dense",
    )


def back_kernel(
    low, high, adds, takes, cuts, tail, idle, plan_ref, grads_ref, adj_ref, *refs
):
    received, refs = refs[: len(adds)], refs[len(adds) :]
    tails, refs = refs[: len(takes)], refs[len(takes) :]
    outs, sum_ref = refs[idle + 1 :], refs[-1]
    slots = adj_ref.shape[0]
    total = sum_ref.shape[0] - 1
    blocks = total // (high - low)
    sum_ref[...] = jnp.zeros_like(sum_ref)
    for (at, rows, skip), ref in zip(adds, received):
        sum_ref[at : at + rows] += ref[skip : skip + rows].astype(jnp.float32)

    def add(spot, valid):
        slot, _, col, key, place = fields(plan_ref[spot])
        back = lax.dot_general(
            grads_ref[place], adj_ref[slot], NT, preferred_element_type=jnp.float32
        )
        spot = jnp.where(valid, (key - (low & 7)) * blocks + col - (low & 8) * blocks, total)
        sum_ref[spot] += back.astype(jnp.bfloat16).astype(jnp.float32)

    ranged(plan_ref[slots + low], plan_ref[slots + high], add)
    at = 0
    for (rows, with_tail), out in zip(cuts, outs):
        out[:rows] = sum_ref[at : at + rows].astype(out.dtype)
        at += rows
    if tail:
        if len(tails) == 1 and not takes[0]:
            chunks = tails[0]
            value = sum(
                chunks[k, -2:].astype(jnp.float32) for k in range(chunks.shape[0])
            )
        else:
            value = sum(
                ref[at : at + 2].astype(jnp.float32) for at, ref in zip(takes, tails)
            )
        value = value.astype(jnp.bfloat16)
        outs[len(cuts)][...] = value
        for (rows, with_tail), out in zip(cuts, outs):
            if with_tail:
                out[rows:] = value


def back_stage(plan, grads, adj, low, high, cuts, received=(), tails=(), idle=()):
    slots, width, _ = adj.shape
    cols = grads.shape[1]
    blocks = sum(rows for rows, _, _ in cuts) // (high - low)
    shapes = [
        jax.ShapeDtypeStruct((rows + (2 if with_tail else 0), cols, width), dtype)
        for rows, dtype, with_tail in cuts
    ]
    if tails:
        shapes.append(jax.ShapeDtypeStruct((2, cols, width), jnp.bfloat16))
    kept = jax.ShapeDtypeStruct(adj.shape, adj.dtype)
    count = 3 + len(received) + len(tails)
    return call(
        functools.partial(
            back_kernel,
            low,
            high,
            tuple((at, rows, sum(skip)) for at, rows, _, *skip in received),
            tuple(at for at, _ in tails),
            tuple((rows, with_tail) for rows, _, with_tail in cuts),
            len(tails) > 0,
            len(idle),
        ),
        [kept] + shapes + [jax.ShapeDtypeStruct(v.shape, v.dtype) for v in idle],
        (grads, adj, *[entry[2] for entry in received], *[v for _, v in tails]),
        (plan,),
        [pltpu.VMEM(((high - low) * blocks + 1, cols, width), jnp.float32)],
        aliases={2: 0, **{count + i: 1 + len(shapes) + i for i in range(len(idle))}},
        flops=2 * (high - low) * 8 * width**3,
        name="transposed_sums",
        idle=idle,
        idle_out=len(idle),
    )


def relay_kernel(
    z_more_ref, y_own_ref, y_more_ref, y_less_ref, z_two_ref, own_ref, rest_ref,
    up_ref, over_ref, sum_ref,
):
    rows, cols, width = y_own_ref.shape
    full = jnp.float32
    up = z_more_ref[...] + y_more_ref[...].astype(full)
    up_ref[:rows] = (up + z_two_ref[:rows].astype(full)).astype(jnp.bfloat16)
    up_ref[rows:] = z_two_ref[rows:]
    over_ref[...] = (y_own_ref[...] + y_less_ref[:rows].astype(full)).astype(jnp.bfloat16)
    per = rows // rest_ref.shape[0]
    term = rest_ref[:, 2 * per : 3 * per].reshape(rows, cols, width).astype(full)
    sum_ref[...] = own_ref[...] + term


def relay(*values):
    rows, cols, width = values[0].shape
    sizes = ((rows + 2, jnp.bfloat16), (rows, jnp.bfloat16), (rows, jnp.float32))
    shapes = [jax.ShapeDtypeStruct((n, cols, width), dtype) for n, dtype in sizes]
    return call(relay_kernel, shapes, values, name="relay")


def finish_kernel(
    scale, own_ref, less_ref, more_ref, over_ref, g_ref, down_ref, up_ref, input_ref, gs_ref, gn_ref
):
    blocks = own_ref.shape[0]
    full = jnp.float32
    back = own_ref[...] + less_ref[...].astype(full)
    back = back + more_ref[:blocks].astype(full) + over_ref[...].astype(full)
    input_ref[...] = back.astype(jnp.bfloat16)
    total = g_ref[...].astype(full) + more_ref[blocks:].astype(full)
    total = total + (down_ref[blocks:].astype(full) + up_ref[blocks:].astype(full))
    total = total * scale
    gs_ref[...] = total[0]
    gn_ref[...] = total[1]


def finish(scale, *values):
    blocks, cols, width = values[0].shape
    moved = jax.ShapeDtypeStruct((blocks, cols, width), jnp.bfloat16)
    grad = jax.ShapeDtypeStruct((cols, width), jnp.float32)
    return call(
        functools.partial(finish_kernel, scale), [moved, grad, grad], values, name="finish"
    )


def make_plan(tile_row, tile_owner, tile_col, tile_count, blocks):
    slots = tile_row.shape[0]
    ids = jnp.arange(slots, dtype=jnp.int32)
    me = lax.axis_index("blk").astype(jnp.int32)
    owner = tile_owner[:, 0]
    code = ((owner ^ me) >> 3) * 4 + (((owner >> 1) - (me >> 1)) & 3)
    view = sum(jnp.where(code == k, VIEW[k], 0) for k in range(8))
    key = view + 8 * ((owner ^ me) & 1)
    key = jnp.where(ids < tile_count[0], key, 16)
    moved = tile_row + 8 * (tile_row // 3)
    item = ids + (tile_row << 7) + (tile_col << 12) + ((key & 15) << 17) + (moved << 21)
    full = key * slots + ids
    rank = jnp.sum((full[None, :] < full[:, None]).astype(jnp.int32), axis=1)
    ordered = jnp.sum(jnp.where(rank[None, :] == ids[:, None], item[None, :], 0), axis=1)
    starts = jnp.sum((key[None, :] < jnp.arange(32, dtype=jnp.int32)[:, None]).astype(jnp.int32), axis=1)
    here = jnp.full((8,), lax.axis_index("col"), jnp.int32)
    rows = jnp.where(ids < tile_count[0], tile_row, blocks)
    return jnp.concatenate([ordered, starts, here, rows])


def local(
    features, cotangent, w_self, w_neigh, tile_row, tile_owner, tile_col, tile_count,
    edge_dst, edge_src,
):
    blocks, cols, width = features.shape
    n_blk, n_col = lax.axis_size("blk"), lax.axis_size("col")
    per = blocks // n_col
    third = blocks // 3

    def over_col(a, rows):
        moved = lax.all_to_all(a.reshape(n_col, rows * cols, width), "col", 0, 0)
        return moved.reshape(n_col, rows, cols, width)

    own = features
    z_less, z_more, y_own = send(own, "up"), send(own, "down"), send(own, "over")
    plan = make_plan(tile_row, tile_owner, tile_col, tile_count, blocks)
    build = functools.partial(
        adjacency, plan=plan, edges=edge_src + (edge_dst << 8), blocks=blocks, width=width
    )
    adj, deg, turn = build(0, weights=jnp.stack([w_self, w_neigh]))
    deg, near, z_more, y_own = join_near((own, z_less, z_more, y_own), deg)
    y_more, y_less, z_two = send(z_more, "over"), send(y_own, "up"), send(z_more, "down")
    near_swap = send(near, "core")
    adj, deg, inverse = build(1, state=(adj, deg))
    inverse, mid, *cut = join_mid((y_more, y_less, z_two), inverse)
    cut = [send(cut[0], "over"), send(cut[1], "up"), send(cut[2], "down")]
    mid_swap = send(mid, "core")
    sums = mean_stage(plan, adj, 0, 4, [near, near_swap], idle=(mid,))
    sums, y_two = join_far(cut, sums)
    y_swap = send(y_two, "core")
    sums = mean_stage(plan, adj, 4, 7, [mid, mid_swap], sums)
    packed = mean_stage(
        plan, adj, 7, 8, [y_two, y_swap], sums, (inverse, own, cotangent), n_col
    )

    out, adj = dense(plan, over_col(packed, 3 * per), turn, inverse, adj)
    moved = over_col(out, 3 * per + 2)
    hidden = moved[:, per : 2 * per].reshape(blocks, cols, width)
    grads = moved.reshape(n_col * (3 * per + 2), cols, width)

    half, full = jnp.bfloat16, jnp.float32
    back = functools.partial(back_stage, plan, grads)
    adj, far, g = back(adj, 12, 16, [(4 * blocks, half, True)], tails=[(0, moved)])
    far = send(far, "core")
    adj, near = back(adj, 8, 12, [(4 * blocks, half, False)])
    near = send(near, "core")
    adj, *cut, g = back(
        adj, 7, 8, [(third, half, True), (third, half, False), (third, half, False)],
        [(0, blocks, far, 3 * blocks)], [(0, g), (4 * blocks, far)],
    )
    cut = [send(cut[0], "over"), send(cut[1], "down"), send(cut[2], "up")]
    adj, own, z_less, z_more, y_own = back(
        adj, 0, 4,
        [(blocks, full, False), (blocks, half, False), (blocks, full, False), (blocks, full, False)],
        [(0, 4 * blocks, near)],
    )
    z_less = send(z_less, "down")
    adj, y_more, y_less, z_two, g = back(
        adj, 4, 7, [(blocks, half, False), (blocks, half, True), (blocks, half, True)],
        [(0, 3 * blocks, far), (2 * blocks, third, cut[0]), (blocks + third, third, cut[1]),
         (2 * third, third, cut[2])],
        [(0, g), (third, cut[0])],
    )
    y_more, y_less, z_two = send(y_more, "over"), send(y_less, "down"), send(z_two, "up")
    z_more, y_own, own = relay(z_more, y_own, y_more, y_less, z_two, own, moved)
    z_more, y_own = send(z_more, "up"), send(y_own, "over")
    scale = 1.0 / math.sqrt(blocks * width * n_blk)
    return (hidden, *finish(scale, own, z_less, z_more, y_own, g, y_less, z_two))


def solution(mesh):
    placed = (
        P("blk", "col", None),
        P("blk", "col", None),
        P(),
        P(),
        P("blk"),
        P("blk", None),
        P("blk"),
        P("blk"),
        P("blk", None),
        P("blk", None),
    )
    return jax.shard_map(
        local,
        mesh=mesh,
        in_specs=placed,
        out_specs=(P("blk", "col", None), P("blk", "col", None), P("col", None), P("col", None)),
        check_vma=False,
    )
```

```python
import functools
import math

import jax
import jax.numpy as jnp
from jax import lax
from jax.experimental import pallas as pl
from jax.experimental.pallas import tpu as pltpu
from jax.sharding import PartitionSpec as P

UNROLL = 12
HERE = 160
ROWS = 168
CUTS = (0, 4, 16)
VMEM_BYTES = 14 * 1024 * 1024
NT = (((1,), (1,)), ((), ()))
WHOLE = pl.BlockSpec(memory_space=pltpu.VMEM)
IDLE = pl.BlockSpec(memory_space=pl.ANY)

VIEW = (0, 2, 6, 1, 3, 4, 7, 5)


def turned(i, dz):
    y, z, core = i >> 3, (i >> 1) & 3, i & 1
    return (y << 3) | (((z + dz) % 4) << 1) | core


ROUTES = {
    "up": [(i, turned(i, 1)) for i in range(16)],
    "down": [(i, turned(i, -1)) for i in range(16)],
    "over": [(i, i ^ 8) for i in range(16)],
    "core": [(i, i ^ 1) for i in range(16)],
}


def send(value, route):
    return lax.ppermute(value, "blk", ROUTES[route])


def with_plan(kernel, plan_ref, *refs):
    *refs, held_ref, sem = refs
    copy = pltpu.make_async_copy(plan_ref, held_ref, sem)
    copy.start()
    kernel(held_ref, copy.wait, *refs)


def call(
    kernel, out_shape, operands, plan=None, scratch=(), aliases=None, name=None, idle=(), idle_out=0
):
    scratch = list(scratch)
    if plan is not None:
        kernel = functools.partial(with_plan, kernel)
        scratch += [pltpu.SMEM(plan.shape, plan.dtype), pltpu.SemaphoreType.DMA]
    lead = [] if plan is None else [plan]
    return pl.pallas_call(
        kernel,
        in_specs=[IDLE] * len(lead) + [WHOLE] * len(operands) + [IDLE] * len(idle),
        out_specs=[WHOLE] * (len(out_shape) - idle_out) + [IDLE] * idle_out,
        out_shape=out_shape,
        scratch_shapes=scratch,
        input_output_aliases=aliases or {},
        compiler_params=pltpu.CompilerParams(vmem_limit_bytes=VMEM_BYTES),
        name=name,
    )(*lead, *operands, *idle)


def one_hot(ids, lanes):
    one, zero = jnp.ones((), jnp.float8_e4m3fn), jnp.zeros((), jnp.float8_e4m3fn)
    return jnp.where(lanes == ids, one, zero)


def adjacency_kernel(first, last, fresh, final, plan_ref, ready, edge_ref, *refs):
    if not fresh:
        refs = refs[2:]
    adj_ref, deg_ref, refs = refs[0], refs[1], refs[2:]
    width = adj_ref.shape[1]
    edges = edge_ref.shape[1]
    if fresh:
        deg_ref[...] = jnp.zeros_like(deg_ref)
    lanes = lax.broadcasted_iota(jnp.int32, (width, edges), 0).astype(jnp.int8)
    ready()

    def body(i, carry):
        base = pl.multiple_of(i * 8, 8)
        both = edge_ref[pl.ds(base, 8), :]
        src, dst = (both & 255).astype(jnp.int8), (both >> 8).astype(jnp.int8)
        for j in range(8):
            spread, collect = one_hot(src[j : j + 1], lanes), one_hot(dst[j : j + 1], lanes)
            adj = lax.dot_general(spread, collect, NT, preferred_element_type=jnp.float32)
            adj_ref[base + j] = adj.astype(jnp.bfloat16)
            deg_ref[plan_ref[ROWS + base + j]] += jnp.sum(adj.reshape(width // 8, 8, width), axis=0)
        return carry

    lax.fori_loop(first, last, body, 0)
    if final:
        inv_ref = refs[0]
        blocks = inv_ref.shape[0]
        degree = jnp.sum(deg_ref[:blocks], axis=1, keepdims=True)
        inv_ref[...] = 1.0 / jnp.maximum(degree, 1.0)


def adjacency(k, plan, edges, blocks, width, state=()):
    slots, count = edges.shape
    fresh, final = k == 0, k == len(CUTS) - 2
    outs = [
        jax.ShapeDtypeStruct((slots, width, width), jnp.bfloat16),
        jax.ShapeDtypeStruct((blocks + 1, 8, width), jnp.float32),
    ]
    if final:
        outs.append(jax.ShapeDtypeStruct((blocks, 1, width), jnp.float32))
    return call(
        functools.partial(adjacency_kernel, CUTS[k], CUTS[k + 1], fresh, final),
        outs,
        (edges, *state),
        plan,
        aliases=None if fresh else {2: 0, 3: 1},
        name="adjacency",
    )


def near_kernel(own_ref, less_ref, more_ref, over_ref, kept_ref, deg_ref, near_ref, one_ref, two_ref):
    rows = own_ref.shape[0]
    for k, ref in enumerate((own_ref, less_ref, more_ref, over_ref)):
        near_ref[k * rows : (k + 1) * rows] = ref[...]
    one_ref[...] = more_ref[...]
    two_ref[...] = over_ref[...]


def join_near(pieces, deg):
    rows, cols, width = pieces[0].shape
    return call(
        near_kernel,
        [jax.ShapeDtypeStruct(deg.shape, deg.dtype)]
        + [jax.ShapeDtypeStruct((n, cols, width), jnp.bfloat16) for n in (4 * rows, rows, rows)],
        (*pieces, deg),
        aliases={4: 0},
        name="join",
    )


def mid_kernel(more_ref, less_ref, two_ref, kept_ref, sum_ref, mid_ref, *outs):
    rows = more_ref.shape[0]
    third = rows // 3
    for k, ref in enumerate((more_ref, less_ref, two_ref)):
        mid_ref[k * rows : (k + 1) * rows] = ref[...]
    outs[0][...] = two_ref[:third]
    outs[1][...] = less_ref[third : 2 * third]
    outs[2][...] = more_ref[2 * third :]


def join_mid(pieces, kept):
    rows, cols, width = pieces[0].shape
    sizes = (3 * rows,) + (rows // 3,) * 3
    return call(
        mid_kernel,
        [jax.ShapeDtypeStruct(kept.shape, kept.dtype)]
        + [jax.ShapeDtypeStruct((n, cols, width), jnp.bfloat16) for n in sizes],
        (*pieces, kept),
        aliases={3: 0},
        name="join",
    )


def far_kernel(one_ref, two_ref, three_ref, kept_ref, sum_ref, far_ref):
    rows = one_ref.shape[0]
    for k, ref in enumerate((one_ref, two_ref, three_ref)):
        far_ref[k * rows : (k + 1) * rows] = ref[...]


def join_far(pieces, sums):
    rows, cols, width = pieces[0].shape
    return call(
        far_kernel,
        [
            jax.ShapeDtypeStruct(sums.shape, sums.dtype),
            jax.ShapeDtypeStruct((3 * rows, cols, width), jnp.bfloat16),
        ],
        (*pieces, sums),
        aliases={3: 0},
        name="join",
    )


def ranged(start, stop, body):
    def step(i, carry):
        for j in range(UNROLL):
            spot = start + i * UNROLL + j
            body(jnp.minimum(spot, stop - 1), spot < stop)
        return carry

    lax.fori_loop(0, (stop - start + UNROLL - 1) // UNROLL, step, 0)


def fields(item):
    return item & 127, (item >> 7) & 31, (item >> 12) & 31, (item >> 17) & 15, item >> 21


def mean_kernel(low, high, fresh, final, turns, idle, plan_ref, ready, adj_ref, here_ref, swap_ref, *refs):
    if not fresh:
        refs = refs[1:]
    if final:
        inv_ref, x_ref, cot_ref, refs = *refs[:3], refs[3:]
    if turns:
        weight_ref, refs = refs[0], refs[1 + idle :]
        for k in range(2):
            refs[1][k] = weight_ref[k]
            refs[1][2 + k] = weight_ref[k].T
    sum_ref = refs[0]
    blocks = sum_ref.shape[0] - 1
    slots = adj_ref.shape[0]
    if fresh:
        sum_ref[...] = jnp.zeros_like(sum_ref)
    if final:
        out_ref = refs[1]
        parts, rows, cols, width = out_ref.shape
        rows = rows // 3
        out_ref[:, rows : 2 * rows] = x_ref[...].reshape(parts, rows, cols, width)
        out_ref[:, 2 * rows :] = cot_ref[...].reshape(parts, rows, cols, width)
    ready()

    for core, feats_ref in enumerate((here_ref, swap_ref)):
        def add(spot, valid):
            slot, row, col, key, _ = fields(plan_ref[spot])
            place = (key - low - 8 * core) * blocks + col
            flow = jnp.dot(feats_ref[place], adj_ref[slot], preferred_element_type=jnp.float32)
            sum_ref[jnp.where(valid, row, blocks)] += flow

        ranged(plan_ref[slots + low + 8 * core], plan_ref[slots + high + 8 * core], add)
    if final:
        mean = (sum_ref[:blocks] * inv_ref[...]).astype(jnp.bfloat16)
        out_ref[:, :rows] = mean.reshape(parts, rows, cols, width)


def mean_stage(plan, adj, low, high, pieces, before=None, last=(), parts=0, weights=None, idle=()):
    rows, cols, width = pieces[0].shape
    blocks = rows // (high - low)
    fresh, final = before is None, len(last) > 0
    outs = [jax.ShapeDtypeStruct((blocks + 1, cols, width), jnp.float32)]
    if final:
        outs.append(jax.ShapeDtypeStruct((parts, 3 * blocks // parts, cols, width), jnp.bfloat16))
    turns = weights is not None
    if turns:
        outs.append(jax.ShapeDtypeStruct((4,) + weights.shape[1:], jnp.bfloat16))
    return call(
        functools.partial(mean_kernel, low, high, fresh, final, turns, len(idle)),
        outs,
        [adj, *pieces] + ([] if fresh else [before]) + list(last) + ([weights] if turns else []),
        plan,
        aliases=None if fresh else {4: 0},
        idle=idle,
        name="neighbor_mean",
    )


def dense_kernel(plan_ref, ready, in_ref, turn_ref, inv_ref, adj_ref, out_ref, kept_ref, gs_ref, gn_ref):
    parts, rows, cols, width = in_ref.shape
    rows = rows // 3
    feats = parts * cols
    ready()
    here = plan_ref[HERE]
    for i in range(rows):
        mean = in_ref[:, i].reshape(feats, width)
        x = in_ref[:, rows + i].reshape(feats, width)
        cot = in_ref[:, 2 * rows + i].reshape(feats, width).astype(jnp.float32)
        preact = jnp.dot(turn_ref[2], x, preferred_element_type=jnp.float32)
        preact = preact + jnp.dot(turn_ref[3], mean, preferred_element_type=jnp.float32)
        gate = jax.nn.sigmoid(preact)
        hidden = (preact * gate).astype(jnp.bfloat16)
        out_ref[:, rows + i] = hidden.reshape(parts, cols, width)
        out_grad = (cot * gate * (1.0 + preact * (1.0 - gate))).astype(jnp.bfloat16)
        self_term = jnp.dot(turn_ref[0], out_grad, preferred_element_type=jnp.float32)
        out_ref[:, 2 * rows + i] = self_term.astype(jnp.bfloat16).reshape(parts, cols, width)
        pre = jnp.dot(turn_ref[1], out_grad, preferred_element_type=jnp.float32)
        pre = pre * inv_ref[here * rows + i]
        out_ref[:, i] = pre.astype(jnp.bfloat16).reshape(parts, cols, width)
        for ref, left in ((gs_ref, x), (gn_ref, mean)):
            term = lax.dot_general(left, out_grad, NT, preferred_element_type=jnp.float32)
            ref[...] = ref[...] + term if i else term
    for k, ref in enumerate((gs_ref, gn_ref)):
        out_ref[:, 3 * rows + k] = ref[...].astype(jnp.bfloat16).reshape(parts, cols, width)


def dense(plan, packed, turn, inverse, adj):
    parts, rows, cols, width = packed.shape
    feats = parts * cols
    grad = pltpu.VMEM((feats, feats), jnp.float32)
    return call(
        dense_kernel,
        [
            jax.ShapeDtypeStruct((parts, rows + 2, cols, width), jnp.bfloat16),
            jax.ShapeDtypeStruct(adj.shape, adj.dtype),
        ],
        (packed, turn, inverse, adj),
        plan,
        [grad, grad],
        aliases={4: 1},
        name="dense",
    )


def back_kernel(
    low, high, adds, takes, cuts, tail, idle, plan_ref, ready, grads_ref, adj_ref, *refs
):
    received, refs = refs[: len(adds)], refs[len(adds) :]
    tails, refs = refs[: len(takes)], refs[len(takes) :]
    outs, sum_ref = refs[idle + 1 :], refs[-1]
    slots = adj_ref.shape[0]
    total = sum_ref.shape[0] - 1
    blocks = total // (high - low)
    sum_ref[...] = jnp.zeros_like(sum_ref)
    for (at, rows, skip), ref in zip(adds, received):
        sum_ref[at : at + rows] += ref[skip : skip + rows].astype(jnp.float32)

    ready()

    def add(spot, valid):
        slot, _, col, key, place = fields(plan_ref[spot])
        back = lax.dot_general(
            grads_ref[place], adj_ref[slot], NT, preferred_element_type=jnp.float32
        )
        spot = jnp.where(valid, (key - (low & 7)) * blocks + col - (low & 8) * blocks, total)
        sum_ref[spot] += back.astype(jnp.bfloat16).astype(jnp.float32)

    ranged(plan_ref[slots + low], plan_ref[slots + high], add)
    at = 0
    for (rows, with_tail), out in zip(cuts, outs):
        out[:rows] = sum_ref[at : at + rows].astype(out.dtype)
        at += rows
    if tail:
        if len(tails) == 1 and not takes[0]:
            chunks = tails[0]
            value = sum(
                chunks[k, -2:].astype(jnp.float32) for k in range(chunks.shape[0])
            )
        else:
            value = sum(
                ref[at : at + 2].astype(jnp.float32) for at, ref in zip(takes, tails)
            )
        value = value.astype(jnp.bfloat16)
        outs[len(cuts)][...] = value
        for (rows, with_tail), out in zip(cuts, outs):
            if with_tail:
                out[rows:] = value


def back_stage(plan, grads, adj, low, high, cuts, received=(), tails=(), idle=(), name=None):
    slots, width, _ = adj.shape
    cols = grads.shape[1]
    blocks = sum(rows for rows, _, _ in cuts) // (high - low)
    shapes = [
        jax.ShapeDtypeStruct((rows + (2 if with_tail else 0), cols, width), dtype)
        for rows, dtype, with_tail in cuts
    ]
    if tails:
        shapes.append(jax.ShapeDtypeStruct((2, cols, width), jnp.bfloat16))
    kept = jax.ShapeDtypeStruct(adj.shape, adj.dtype)
    count = 3 + len(received) + len(tails)
    return call(
        functools.partial(
            back_kernel,
            low,
            high,
            tuple((at, rows, sum(skip)) for at, rows, _, *skip in received),
            tuple(at for at, _ in tails),
            tuple((rows, with_tail) for rows, _, with_tail in cuts),
            len(tails) > 0,
            len(idle),
        ),
        [kept] + shapes + [jax.ShapeDtypeStruct(v.shape, v.dtype) for v in idle],
        (grads, adj, *[entry[2] for entry in received], *[v for _, v in tails]),
        plan,
        [pltpu.VMEM(((high - low) * blocks + 1, cols, width), jnp.float32)],
        aliases={2: 0, **{count + i: 1 + len(shapes) + i for i in range(len(idle))}},
        name=name,
        idle=idle,
        idle_out=len(idle),
    )


def relay_kernel(
    z_more_ref, y_own_ref, y_more_ref, y_less_ref, z_two_ref, own_ref, rest_ref,
    up_ref, over_ref, sum_ref,
):
    rows, cols, width = y_own_ref.shape
    full = jnp.float32
    up = z_more_ref[...] + y_more_ref[...].astype(full)
    up_ref[:rows] = (up + z_two_ref[:rows].astype(full)).astype(jnp.bfloat16)
    up_ref[rows:] = z_two_ref[rows:]
    over_ref[...] = (y_own_ref[...] + y_less_ref[:rows].astype(full)).astype(jnp.bfloat16)
    per = rows // rest_ref.shape[0]
    term = rest_ref[:, 2 * per : 3 * per].reshape(rows, cols, width).astype(full)
    sum_ref[...] = own_ref[...] + term


def relay(*values):
    rows, cols, width = values[0].shape
    sizes = ((rows + 2, jnp.bfloat16), (rows, jnp.bfloat16), (rows, jnp.float32))
    shapes = [jax.ShapeDtypeStruct((n, cols, width), dtype) for n, dtype in sizes]
    return call(relay_kernel, shapes, values, name="relay")


def finish_kernel(
    scale, own_ref, less_ref, more_ref, over_ref, g_ref, down_ref, up_ref, input_ref, gs_ref, gn_ref
):
    blocks = own_ref.shape[0]
    full = jnp.float32
    back = own_ref[...] + less_ref[...].astype(full)
    back = back + more_ref[:blocks].astype(full) + over_ref[...].astype(full)
    input_ref[...] = back.astype(jnp.bfloat16)
    total = g_ref[...].astype(full) + more_ref[blocks:].astype(full)
    total = total + (down_ref[blocks:].astype(full) + up_ref[blocks:].astype(full))
    total = total * scale
    gs_ref[...] = total[0]
    gn_ref[...] = total[1]


def finish(scale, *values):
    blocks, cols, width = values[0].shape
    moved = jax.ShapeDtypeStruct((blocks, cols, width), jnp.bfloat16)
    grad = jax.ShapeDtypeStruct((cols, width), jnp.float32)
    return call(
        functools.partial(finish_kernel, scale), [moved, grad, grad], values, name="finish"
    )


def make_plan(tile_row, tile_owner, tile_col, tile_count, blocks):
    slots = tile_row.shape[0]
    ids = jnp.arange(slots, dtype=jnp.int32)
    me = lax.axis_index("blk").astype(jnp.int32)
    owner = tile_owner[:, 0]
    code = ((owner ^ me) >> 3) * 4 + (((owner >> 1) - (me >> 1)) & 3)
    view = sum(jnp.where(code == k, VIEW[k], 0) for k in range(8))
    key = view + 8 * ((owner ^ me) & 1)
    key = jnp.where(ids < tile_count[0], key, 16)
    moved = tile_row + 8 * (tile_row // 3)
    item = ids + (tile_row << 7) + (tile_col << 12) + ((key & 15) << 17) + (moved << 21)
    full = key * slots + ids
    rank = jnp.sum((full[None, :] < full[:, None]).astype(jnp.int32), axis=1)
    ordered = jnp.sum(jnp.where(rank[None, :] == ids[:, None], item[None, :], 0), axis=1)
    starts = jnp.sum((key[None, :] < jnp.arange(32, dtype=jnp.int32)[:, None]).astype(jnp.int32), axis=1)
    here = jnp.full((8,), lax.axis_index("col"), jnp.int32)
    rows = jnp.where(ids < tile_count[0], tile_row, blocks)
    return jnp.concatenate([ordered, starts, here, rows])


def local(
    features, cotangent, w_self, w_neigh, tile_row, tile_owner, tile_col, tile_count,
    edge_dst, edge_src,
):
    blocks, cols, width = features.shape
    n_blk, n_col = lax.axis_size("blk"), lax.axis_size("col")
    per = blocks // n_col
    third = blocks // 3

    def over_col(a, rows):
        moved = lax.all_to_all(a.reshape(n_col, rows * cols, width), "col", 0, 0)
        return moved.reshape(n_col, rows, cols, width)

    own = features
    z_less, z_more, y_own = send(own, "up"), send(own, "down"), send(own, "over")
    plan = make_plan(tile_row, tile_owner, tile_col, tile_count, blocks)
    build = functools.partial(
        adjacency, plan=plan, edges=edge_src + (edge_dst << 8), blocks=blocks, width=width
    )
    adj, deg = build(0)
    deg, near, z_more, y_own = join_near((own, z_less, z_more, y_own), deg)
    y_more, y_less, z_two = send(z_more, "over"), send(y_own, "up"), send(z_more, "down")
    near_swap = send(near, "core")
    adj, deg, inverse = build(1, state=(adj, deg))
    inverse, mid, *cut = join_mid((y_more, y_less, z_two), inverse)
    cut = [send(cut[0], "over"), send(cut[1], "up"), send(cut[2], "down")]
    mid_swap = send(mid, "core")
    sums, turn = mean_stage(
        plan, adj, 0, 4, [near, near_swap], weights=jnp.stack([w_self, w_neigh]), idle=(mid,)
    )
    sums, y_two = join_far(cut, sums)
    y_swap = send(y_two, "core")
    (sums,) = mean_stage(plan, adj, 4, 7, [mid, mid_swap], sums)
    _, packed = mean_stage(
        plan, adj, 7, 8, [y_two, y_swap], sums, (inverse, own, cotangent), n_col
    )

    out, adj = dense(plan, over_col(packed, 3 * per), turn, inverse, adj)
    moved = over_col(out, 3 * per + 2)
    hidden = moved[:, per : 2 * per].reshape(blocks, cols, width)
    grads = moved.reshape(n_col * (3 * per + 2), cols, width)

    half, full = jnp.bfloat16, jnp.float32
    back = functools.partial(back_stage, plan, grads)
    adj, far, g = back(adj, 15, 16, name="sums_far_swap", cuts=[(blocks, half, True)], tails=[(0, moved)])
    far = send(far, "core")
    adj, mid = back(adj, 12, 15, name="sums_mid_swap", cuts=[(3 * blocks, half, False)])
    adj, *cut, g, mid = back(
        adj, 7, 8, name="sums_far_own", cuts=[(third, half, True), (third, half, False), (third, half, False)],
        received=[(0, blocks, far)], tails=[(0, g), (blocks, far)], idle=(mid,),
    )
    mid = send(mid, "core")
    cut = [send(cut[0], "over"), send(cut[1], "down"), send(cut[2], "up")]
    adj, near = back(adj, 8, 12, name="sums_near_swap", cuts=[(4 * blocks, half, False)])
    adj, y_more, y_less, z_two, g, near = back(
        adj, 4, 7, name="sums_mid_own", cuts=[(blocks, half, False), (blocks, half, True), (blocks, half, True)],
        received=[(0, 3 * blocks, mid), (2 * blocks, third, cut[0]), (blocks + third, third, cut[1]),
         (2 * third, third, cut[2])],
        tails=[(0, g), (third, cut[0])], idle=(near,),
    )
    near = send(near, "core")
    y_more, y_less, z_two = send(y_more, "over"), send(y_less, "down"), send(z_two, "up")
    adj, own, z_less, z_more, y_own = back(
        adj, 0, 4, name="sums_near_own", cuts=
        [(blocks, full, False), (blocks, half, False), (blocks, full, False), (blocks, full, False)],
        received=[(0, 4 * blocks, near)],
    )
    z_less = send(z_less, "down")
    z_more, y_own, own = relay(z_more, y_own, y_more, y_less, z_two, own, moved)
    z_more, y_own = send(z_more, "up"), send(y_own, "over")
    scale = 1.0 / math.sqrt(blocks * width * n_blk)
    return (hidden, *finish(scale, own, z_less, z_more, y_own, g, y_less, z_two))


def solution(mesh):
    placed = (
        P("blk", "col", None),
        P("blk", "col", None),
        P(),
        P(),
        P("blk"),
        P("blk", None),
        P("blk"),
        P("blk"),
        P("blk", None),
        P("blk", None),
    )
    return jax.shard_map(
        local,
        mesh=mesh,
        in_specs=placed,
        out_specs=(P("blk", "col", None), P("blk", "col", None), P("col", None), P("col", None)),
        check_vma=False,
    )
```

```python
import functools
import math

import jax
import jax.numpy as jnp
from jax import lax
from jax.experimental import pallas as pl
from jax.experimental.pallas import tpu as pltpu
from jax.sharding import PartitionSpec as P

UNROLL = 12
HERE = 160
ROWS = 168
CUTS = (0, 11, 16)
VMEM_BYTES = 14 * 1024 * 1024
NT = (((1,), (1,)), ((), ()))
WHOLE = pl.BlockSpec(memory_space=pltpu.VMEM)
IDLE = pl.BlockSpec(memory_space=pl.ANY)

VIEW = (0, 2, 6, 1, 3, 4, 7, 5)


def turned(i, dz):
    y, z, core = i >> 3, (i >> 1) & 3, i & 1
    return (y << 3) | (((z + dz) % 4) << 1) | core


ROUTES = {
    "up": [(i, turned(i, 1)) for i in range(16)],
    "down": [(i, turned(i, -1)) for i in range(16)],
    "over": [(i, i ^ 8) for i in range(16)],
    "core": [(i, i ^ 1) for i in range(16)],
}


def send(value, route):
    return lax.ppermute(value, "blk", ROUTES[route])


def with_plan(kernel, plan_ref, *refs):
    *refs, held_ref, sem = refs
    copy = pltpu.make_async_copy(plan_ref, held_ref, sem)
    copy.start()
    kernel(held_ref, copy.wait, *refs)


def call(
    kernel, out_shape, operands, plan=None, scratch=(), aliases=None, name=None, idle=(), idle_out=0
):
    scratch = list(scratch)
    if plan is not None:
        kernel = functools.partial(with_plan, kernel)
        scratch += [pltpu.SMEM(plan.shape, plan.dtype), pltpu.SemaphoreType.DMA]
    lead = [] if plan is None else [plan]
    return pl.pallas_call(
        kernel,
        in_specs=[IDLE] * len(lead) + [WHOLE] * len(operands) + [IDLE] * len(idle),
        out_specs=[WHOLE] * (len(out_shape) - idle_out) + [IDLE] * idle_out,
        out_shape=out_shape,
        scratch_shapes=scratch,
        input_output_aliases=aliases or {},
        compiler_params=pltpu.CompilerParams(vmem_limit_bytes=VMEM_BYTES),
        name=name,
    )(*lead, *operands, *idle)


def one_hot(ids, lanes):
    one, zero = jnp.ones((), jnp.float8_e4m3fn), jnp.zeros((), jnp.float8_e4m3fn)
    return jnp.where(lanes == ids, one, zero)


def adjacency_kernel(first, last, fresh, final, idle, plan_ref, ready, edge_ref, *refs):
    refs = refs[idle:] if fresh else refs[2 + idle :]
    adj_ref, deg_ref, refs = refs[0], refs[1], refs[2:]
    width = adj_ref.shape[1]
    edges = edge_ref.shape[1]
    if fresh:
        deg_ref[...] = jnp.zeros_like(deg_ref)
    lanes = lax.broadcasted_iota(jnp.int32, (width, edges), 0).astype(jnp.int8)
    ready()

    def body(i, carry):
        base = pl.multiple_of(i * 8, 8)
        both = edge_ref[pl.ds(base, 8), :]
        src, dst = (both & 255).astype(jnp.int8), (both >> 8).astype(jnp.int8)
        for j in range(8):
            spread, collect = one_hot(src[j : j + 1], lanes), one_hot(dst[j : j + 1], lanes)
            adj = lax.dot_general(spread, collect, NT, preferred_element_type=jnp.float32)
            adj_ref[base + j] = adj.astype(jnp.bfloat16)
            deg_ref[plan_ref[ROWS + base + j]] += jnp.sum(adj.reshape(width // 8, 8, width), axis=0)
        return carry

    lax.fori_loop(first, last, body, 0)
    if final:
        inv_ref = refs[0]
        blocks = inv_ref.shape[0]
        degree = jnp.sum(deg_ref[:blocks], axis=1, keepdims=True)
        inv_ref[...] = 1.0 / jnp.maximum(degree, 1.0)


def adjacency(k, plan, edges, blocks, width, state=(), idle=()):
    slots, count = edges.shape
    fresh, final = k == 0, k == len(CUTS) - 2
    outs = [
        jax.ShapeDtypeStruct((slots, width, width), jnp.bfloat16),
        jax.ShapeDtypeStruct((blocks + 1, 8, width), jnp.float32),
    ]
    if final:
        outs.append(jax.ShapeDtypeStruct((blocks, 1, width), jnp.float32))
    return call(
        functools.partial(adjacency_kernel, CUTS[k], CUTS[k + 1], fresh, final, len(idle)),
        outs,
        (edges, *state),
        plan,
        aliases=None if fresh else {2: 0, 3: 1},
        name="adjacency",
        idle=idle,
    )


def copy_all(copies):
    for copy in copies:
        copy.start()
    for copy in copies:
        copy.wait()


def join_kernel(kept_ref, *refs):
    near, mid, (deg_ref, near_ref, mid_ref, *outs), sems = refs[:4], refs[4:7], refs[7:-1], refs[-1]
    rows = mid[0].shape[0]
    third = rows // 3
    copy_all([
        pltpu.make_async_copy(ref, out.at[pl.ds(k * rows, rows)], sems.at[at + k])
        for at, out, pieces in ((0, mid_ref, mid), (3, near_ref, near))
        for k, ref in enumerate(pieces)
    ])
    outs[0][...] = mid_ref[2 * rows : 2 * rows + third]
    outs[1][...] = mid_ref[rows + third : rows + 2 * third]
    outs[2][...] = mid_ref[2 * third : rows]


def join(near, mid, kept):
    rows, cols, width = mid[0].shape
    sizes = (4 * rows, 3 * rows) + (rows // 3,) * 3
    return call(
        join_kernel,
        [jax.ShapeDtypeStruct(kept.shape, kept.dtype)]
        + [jax.ShapeDtypeStruct((n, cols, width), jnp.bfloat16) for n in sizes],
        (kept,),
        scratch=[pltpu.SemaphoreType.DMA((7,))],
        aliases={0: 0},
        idle=(*near, *mid),
        name="join",
    )


def far_kernel(one_ref, two_ref, three_ref, kept_ref, sum_ref, far_ref):
    rows = one_ref.shape[0]
    for k, ref in enumerate((one_ref, two_ref, three_ref)):
        far_ref[k * rows : (k + 1) * rows] = ref[...]


def join_far(pieces, sums):
    rows, cols, width = pieces[0].shape
    return call(
        far_kernel,
        [
            jax.ShapeDtypeStruct(sums.shape, sums.dtype),
            jax.ShapeDtypeStruct((3 * rows, cols, width), jnp.bfloat16),
        ],
        (*pieces, sums),
        aliases={3: 0},
        name="join",
    )


def ranged(start, stop, body):
    def step(i, carry):
        for j in range(UNROLL):
            spot = start + i * UNROLL + j
            body(jnp.minimum(spot, stop - 1), spot < stop)
        return carry

    lax.fori_loop(0, (stop - start + UNROLL - 1) // UNROLL, step, 0)


def fields(item):
    return item & 127, (item >> 7) & 31, (item >> 12) & 31, (item >> 17) & 15, item >> 21


def mean_kernel(low, high, fresh, final, turns, idle, plan_ref, ready, adj_ref, *refs):
    if fresh:
        weight_ref, here_ref, swap_ref, refs = *refs[:3], refs[3 + idle :]
    else:
        here_ref, swap_ref, refs = *refs[:2], refs[2:]
    if not fresh:
        refs = refs[1:]
    if final:
        inv_ref, refs = refs[0], refs[1:]
    if turns:
        for k in range(2):
            refs[1][k] = weight_ref[k]
            refs[1][2 + k] = weight_ref[k].T
    sum_ref = refs[0]
    blocks = sum_ref.shape[0] - 1
    slots = adj_ref.shape[0]
    if fresh:
        copies = [
            pltpu.make_async_copy(a, b, refs[-1].at[k])
            for k, (a, b) in enumerate(zip((here_ref, swap_ref), refs[-3:-1]))
        ]
        for copy in copies:
            copy.start()
        here_ref, swap_ref = refs[-3:-1]
        sum_ref[...] = jnp.zeros_like(sum_ref)
    if final:
        out_ref = refs[1]
        parts, rows, cols, width = out_ref.shape
    ready()

    for core, feats_ref in enumerate((here_ref, swap_ref)):
        if fresh:
            copies[core].wait()

        def add(spot, valid):
            slot, row, col, key, _ = fields(plan_ref[spot])
            place = (key - low - 8 * core) * blocks + col
            flow = jnp.dot(feats_ref[place], adj_ref[slot], preferred_element_type=jnp.float32)
            sum_ref[jnp.where(valid, row, blocks)] += flow

        ranged(plan_ref[slots + low + 8 * core], plan_ref[slots + high + 8 * core], add)
    if final:
        mean = (sum_ref[:blocks] * inv_ref[...]).astype(jnp.bfloat16)
        out_ref[...] = mean.reshape(parts, rows, cols, width)


def mean_stage(plan, adj, low, high, pieces, before=None, last=(), parts=0, weights=None, idle=()):
    rows, cols, width = pieces[0].shape
    blocks = rows // (high - low)
    fresh, final = before is None, len(last) > 0
    outs = [jax.ShapeDtypeStruct((blocks + 1, cols, width), jnp.float32)]
    if final:
        outs.append(jax.ShapeDtypeStruct((parts, blocks // parts, cols, width), jnp.bfloat16))
    turns = weights is not None
    if turns:
        outs.append(jax.ShapeDtypeStruct((4,) + weights.shape[1:], jnp.bfloat16))
    scratch = []
    if fresh:
        scratch = [pltpu.VMEM(pieces[0].shape, jnp.bfloat16)] * 2 + [pltpu.SemaphoreType.DMA((2,))]
    return call(
        functools.partial(mean_kernel, low, high, fresh, final, turns, len(idle)),
        outs,
        [adj, weights] if fresh else [adj, *pieces, before, *last],
        plan,
        scratch,
        aliases=None if fresh else {4: 0},
        idle=(*pieces, *idle) if fresh else (),
        name="neighbor_mean",
    )


def dense_kernel(plan_ref, ready, in_ref, xc_ref, turn_ref, inv_ref, adj_ref, out_ref, kept_ref, gs_ref, gn_ref):
    parts, rows, cols, width = in_ref.shape
    feats = parts * cols
    ready()
    here = plan_ref[HERE]
    for i in range(rows):
        mean = in_ref[:, i].reshape(feats, width)
        x = xc_ref[:, i].reshape(feats, width)
        cot = xc_ref[:, rows + i].reshape(feats, width).astype(jnp.float32)
        preact = jnp.dot(turn_ref[2], x, preferred_element_type=jnp.float32)
        preact = preact + jnp.dot(turn_ref[3], mean, preferred_element_type=jnp.float32)
        gate = jax.nn.sigmoid(preact)
        hidden = (preact * gate).astype(jnp.bfloat16)
        out_ref[:, rows + i] = hidden.reshape(parts, cols, width)
        out_grad = (cot * gate * (1.0 + preact * (1.0 - gate))).astype(jnp.bfloat16)
        self_term = jnp.dot(turn_ref[0], out_grad, preferred_element_type=jnp.float32)
        out_ref[:, 2 * rows + i] = self_term.astype(jnp.bfloat16).reshape(parts, cols, width)
        pre = jnp.dot(turn_ref[1], out_grad, preferred_element_type=jnp.float32)
        pre = pre * inv_ref[here * rows + i]
        out_ref[:, i] = pre.astype(jnp.bfloat16).reshape(parts, cols, width)
        for ref, left in ((gs_ref, x), (gn_ref, mean)):
            term = lax.dot_general(left, out_grad, NT, preferred_element_type=jnp.float32)
            ref[...] = ref[...] + term if i else term
    for k, ref in enumerate((gs_ref, gn_ref)):
        out_ref[:, 3 * rows + k] = ref[...].astype(jnp.bfloat16).reshape(parts, cols, width)


def dense(plan, packed, x_cot, turn, inverse, adj):
    parts, rows, cols, width = packed.shape
    feats = parts * cols
    grad = pltpu.VMEM((feats, feats), jnp.float32)
    return call(
        dense_kernel,
        [
            jax.ShapeDtypeStruct((parts, 3 * rows + 2, cols, width), jnp.bfloat16),
            jax.ShapeDtypeStruct(adj.shape, adj.dtype),
        ],
        (packed, x_cot, turn, inverse, adj),
        plan,
        [grad, grad],
        aliases={5: 1},
        name="dense",
    )


def back_kernel(
    low, high, adds, takes, cuts, tail, idle, plan_ref, ready, grads_ref, adj_ref, *refs
):
    received, refs = refs[: len(adds)], refs[len(adds) :]
    tails, refs = refs[: len(takes)], refs[len(takes) :]
    outs, sum_ref = refs[idle + 1 :], refs[-1]
    slots = adj_ref.shape[0]
    total = sum_ref.shape[0] - 1
    blocks = total // (high - low)
    sum_ref[...] = jnp.zeros_like(sum_ref)
    for (at, rows, skip), ref in zip(adds, received):
        sum_ref[at : at + rows] += ref[skip : skip + rows].astype(jnp.float32)

    ready()

    def add(spot, valid):
        slot, _, col, key, place = fields(plan_ref[spot])
        back = lax.dot_general(
            grads_ref[place], adj_ref[slot], NT, preferred_element_type=jnp.float32
        )
        spot = jnp.where(valid, (key - (low & 7)) * blocks + col - (low & 8) * blocks, total)
        sum_ref[spot] += back.astype(jnp.bfloat16).astype(jnp.float32)

    ranged(plan_ref[slots + low], plan_ref[slots + high], add)
    at = 0
    for (rows, with_tail), out in zip(cuts, outs):
        out[:rows] = sum_ref[at : at + rows].astype(out.dtype)
        at += rows
    if tail:
        if len(tails) == 1 and not takes[0]:
            chunks = tails[0]
            value = sum(
                chunks[k, -2:].astype(jnp.float32) for k in range(chunks.shape[0])
            )
        else:
            value = sum(
                ref[at : at + 2].astype(jnp.float32) for at, ref in zip(takes, tails)
            )
        value = value.astype(jnp.bfloat16)
        outs[len(cuts)][...] = value
        for (rows, with_tail), out in zip(cuts, outs):
            if with_tail:
                out[rows:] = value


def back_stage(plan, grads, adj, low, high, cuts, received=(), tails=(), idle=(), name=None):
    slots, width, _ = adj.shape
    cols = grads.shape[1]
    blocks = sum(rows for rows, _, _ in cuts) // (high - low)
    shapes = [
        jax.ShapeDtypeStruct((rows + (2 if with_tail else 0), cols, width), dtype)
        for rows, dtype, with_tail in cuts
    ]
    if tails:
        shapes.append(jax.ShapeDtypeStruct((2, cols, width), jnp.bfloat16))
    kept = jax.ShapeDtypeStruct(adj.shape, adj.dtype)
    count = 3 + len(received) + len(tails)
    return call(
        functools.partial(
            back_kernel,
            low,
            high,
            tuple((at, rows, sum(skip)) for at, rows, _, *skip in received),
            tuple(at for at, _ in tails),
            tuple((rows, with_tail) for rows, _, with_tail in cuts),
            len(tails) > 0,
            len(idle),
        ),
        [kept] + shapes + [jax.ShapeDtypeStruct(v.shape, v.dtype) for v in idle],
        (grads, adj, *[entry[2] for entry in received], *[v for _, v in tails]),
        plan,
        [pltpu.VMEM(((high - low) * blocks + 1, cols, width), jnp.float32)],
        aliases={2: 0, **{count + i: 1 + len(shapes) + i for i in range(len(idle))}},
        name=name,
        idle=idle,
        idle_out=len(idle),
    )


def relay_kernel(
    z_more_ref, y_own_ref, y_more_ref, y_less_ref, z_two_ref, own_ref, rest_ref,
    up_ref, over_ref, sum_ref,
):
    rows, cols, width = y_own_ref.shape
    full = jnp.float32
    up = z_more_ref[...] + y_more_ref[...].astype(full)
    up_ref[:rows] = (up + z_two_ref[:rows].astype(full)).astype(jnp.bfloat16)
    up_ref[rows:] = z_two_ref[rows:]
    over_ref[...] = (y_own_ref[...] + y_less_ref[:rows].astype(full)).astype(jnp.bfloat16)
    per = rows // rest_ref.shape[0]
    term = rest_ref[:, 2 * per : 3 * per].reshape(rows, cols, width).astype(full)
    sum_ref[...] = own_ref[...] + term


def relay(*values):
    rows, cols, width = values[0].shape
    sizes = ((rows + 2, jnp.bfloat16), (rows, jnp.bfloat16), (rows, jnp.float32))
    shapes = [jax.ShapeDtypeStruct((n, cols, width), dtype) for n, dtype in sizes]
    return call(relay_kernel, shapes, values, name="relay")


def finish_kernel(
    scale, own_ref, less_ref, more_ref, over_ref, g_ref, down_ref, up_ref, input_ref, gs_ref, gn_ref
):
    blocks = own_ref.shape[0]
    full = jnp.float32
    back = own_ref[...] + less_ref[...].astype(full)
    back = back + more_ref[:blocks].astype(full) + over_ref[...].astype(full)
    input_ref[...] = back.astype(jnp.bfloat16)
    total = g_ref[...].astype(full) + more_ref[blocks:].astype(full)
    total = total + (down_ref[blocks:].astype(full) + up_ref[blocks:].astype(full))
    total = total * scale
    gs_ref[...] = total[0]
    gn_ref[...] = total[1]


def finish(scale, *values):
    blocks, cols, width = values[0].shape
    moved = jax.ShapeDtypeStruct((blocks, cols, width), jnp.bfloat16)
    grad = jax.ShapeDtypeStruct((cols, width), jnp.float32)
    return call(
        functools.partial(finish_kernel, scale), [moved, grad, grad], values, name="finish"
    )


def make_plan(tile_row, tile_owner, tile_col, tile_count, blocks):
    slots = tile_row.shape[0]
    ids = jnp.arange(slots, dtype=jnp.int32)
    me = lax.axis_index("blk").astype(jnp.int32)
    owner = tile_owner[:, 0]
    code = ((owner ^ me) >> 3) * 4 + (((owner >> 1) - (me >> 1)) & 3)
    view = sum(jnp.where(code == k, VIEW[k], 0) for k in range(8))
    key = view + 8 * ((owner ^ me) & 1)
    key = jnp.where(ids < tile_count[0], key, 16)
    moved = tile_row + 8 * (tile_row // 3)
    item = ids + (tile_row << 7) + (tile_col << 12) + ((key & 15) << 17) + (moved << 21)
    full = key * slots + ids
    rank = jnp.sum((full[None, :] < full[:, None]).astype(jnp.int32), axis=1)
    ordered = jnp.sum(jnp.where(rank[None, :] == ids[:, None], item[None, :], 0), axis=1)
    starts = jnp.sum((key[None, :] < jnp.arange(32, dtype=jnp.int32)[:, None]).astype(jnp.int32), axis=1)
    here = jnp.full((8,), lax.axis_index("col"), jnp.int32)
    rows = jnp.where(ids < tile_count[0], tile_row, blocks)
    return jnp.concatenate([ordered, starts, here, rows])


def local(
    features, cotangent, w_self, w_neigh, tile_row, tile_owner, tile_col, tile_count,
    edge_dst, edge_src,
):
    blocks, cols, width = features.shape
    n_blk, n_col = lax.axis_size("blk"), lax.axis_size("col")
    per = blocks // n_col
    third = blocks // 3

    def over_col(a, rows):
        moved = lax.all_to_all(a.reshape(n_col, rows * cols, width), "col", 0, 0)
        return moved.reshape(n_col, rows, cols, width)

    own = features
    z_less, z_more, y_own = send(own, "up"), send(own, "down"), send(own, "over")
    plan = make_plan(tile_row, tile_owner, tile_col, tile_count, blocks)
    build = functools.partial(
        adjacency, plan=plan, edges=edge_src + (edge_dst << 8), blocks=blocks, width=width
    )
    x_cot = over_col(
        jnp.concatenate([a.reshape(n_col, per, cols, width) for a in (features, cotangent)], axis=1),
        2 * per,
    )
    y_more, y_less, z_two = send(z_more, "over"), send(y_own, "up"), send(z_more, "down")
    adj, deg = build(0, idle=(x_cot,))
    deg, near, mid, *cut = join((own, z_less, z_more, y_own), (y_more, y_less, z_two), deg)
    near_swap = send(near, "core")
    cut = [send(cut[0], "over"), send(cut[1], "up"), send(cut[2], "down")]
    mid_swap = send(mid, "core")
    adj, deg, inverse = build(1, state=(adj, deg))
    sums, turn = mean_stage(
        plan, adj, 0, 4, [near, near_swap], weights=jnp.stack([w_self, w_neigh]), idle=(mid,)
    )
    sums, y_two = join_far(cut, sums)
    y_swap = send(y_two, "core")
    (sums,) = mean_stage(plan, adj, 4, 7, [mid, mid_swap], sums)
    _, packed = mean_stage(
        plan, adj, 7, 8, [y_two, y_swap], sums, (inverse,), n_col
    )

    out, adj = dense(plan, over_col(packed, per), x_cot, turn, inverse, adj)
    moved = over_col(out, 3 * per + 2)
    hidden = moved[:, per : 2 * per].reshape(blocks, cols, width)
    grads = moved.reshape(n_col * (3 * per + 2), cols, width)

    half, full = jnp.bfloat16, jnp.float32
    back = functools.partial(back_stage, plan, grads)
    adj, far, g = back(adj, 15, 16, name="sums_far_swap", cuts=[(blocks, half, True)], tails=[(0, moved)])
    far = send(far, "core")
    adj, mid = back(adj, 12, 15, name="sums_mid_swap", cuts=[(3 * blocks, half, False)])
    adj, *cut, g, mid = back(
        adj, 7, 8, name="sums_far_own", cuts=[(third, half, True), (third, half, False), (third, half, False)],
        received=[(0, blocks, far)], tails=[(0, g), (blocks, far)], idle=(mid,),
    )
    mid = send(mid, "core")
    cut = [send(cut[0], "over"), send(cut[1], "down"), send(cut[2], "up")]
    adj, near = back(adj, 8, 12, name="sums_near_swap", cuts=[(4 * blocks, half, False)])
    adj, y_more, y_less, z_two, g, near = back(
        adj, 4, 7, name="sums_mid_own", cuts=[(blocks, half, False), (blocks, half, True), (blocks, half, True)],
        received=[(0, 3 * blocks, mid), (2 * blocks, third, cut[0]), (blocks + third, third, cut[1]),
         (2 * third, third, cut[2])],
        tails=[(0, g), (third, cut[0])], idle=(near,),
    )
    near = send(near, "core")
    y_more, y_less, z_two = send(y_more, "over"), send(y_less, "down"), send(z_two, "up")
    adj, own, z_less, z_more, y_own = back(
        adj, 0, 4, name="sums_near_own", cuts=
        [(blocks, full, False), (blocks, half, False), (blocks, full, False), (blocks, full, False)],
        received=[(0, 4 * blocks, near)],
    )
    z_less = send(z_less, "down")
    z_more, y_own, own = relay(z_more, y_own, y_more, y_less, z_two, own, moved)
    z_more, y_own = send(z_more, "up"), send(y_own, "over")
    scale = 1.0 / math.sqrt(blocks * width * n_blk)
    return (hidden, *finish(scale, own, z_less, z_more, y_own, g, y_less, z_two))


def solution(mesh):
    placed = (
        P("blk", "col", None),
        P("blk", "col", None),
        P(),
        P(),
        P("blk"),
        P("blk", None),
        P("blk"),
        P("blk"),
        P("blk", None),
        P("blk", None),
    )
    return jax.shard_map(
        local,
        mesh=mesh,
        in_specs=placed,
        out_specs=(P("blk", "col", None), P("blk", "col", None), P("col", None), P("col", None)),
        check_vma=False,
    )
```

```python
import functools
import math

import jax
import jax.numpy as jnp
from jax import lax
from jax.experimental import pallas as pl
from jax.experimental.pallas import tpu as pltpu
from jax.sharding import PartitionSpec as P

UNROLL = 12
HERE = 160
ROWS = 168
CUTS = (0, 11, 16)
VMEM_BYTES = 14 * 1024 * 1024
NT = (((1,), (1,)), ((), ()))
WHOLE = pl.BlockSpec(memory_space=pltpu.VMEM)
IDLE = pl.BlockSpec(memory_space=pl.ANY)

VIEW = (0, 2, 6, 1, 3, 4, 7, 5)


def turned(i, dz):
    y, z, core = i >> 3, (i >> 1) & 3, i & 1
    return (y << 3) | (((z + dz) % 4) << 1) | core


ROUTES = {
    "up": [(i, turned(i, 1)) for i in range(16)],
    "down": [(i, turned(i, -1)) for i in range(16)],
    "over": [(i, i ^ 8) for i in range(16)],
    "core": [(i, i ^ 1) for i in range(16)],
}


def send(value, route):
    return lax.ppermute(value, "blk", ROUTES[route])


def with_plan(kernel, plan_ref, *refs):
    *refs, held_ref, sem = refs
    copy = pltpu.make_async_copy(plan_ref, held_ref, sem)
    copy.start()
    kernel(held_ref, copy.wait, *refs)


def call(
    kernel, out_shape, operands, plan=None, scratch=(), aliases=None, name=None, idle=(), idle_out=0
):
    scratch = list(scratch)
    if plan is not None:
        kernel = functools.partial(with_plan, kernel)
        scratch += [pltpu.SMEM(plan.shape, plan.dtype), pltpu.SemaphoreType.DMA]
    lead = [] if plan is None else [plan]
    return pl.pallas_call(
        kernel,
        in_specs=[IDLE] * len(lead) + [WHOLE] * len(operands) + [IDLE] * len(idle),
        out_specs=[WHOLE] * (len(out_shape) - idle_out) + [IDLE] * idle_out,
        out_shape=out_shape,
        scratch_shapes=scratch,
        input_output_aliases=aliases or {},
        compiler_params=pltpu.CompilerParams(vmem_limit_bytes=VMEM_BYTES),
        name=name,
    )(*lead, *operands, *idle)


def one_hot(ids, lanes):
    one, zero = jnp.ones((), jnp.float8_e4m3fn), jnp.zeros((), jnp.float8_e4m3fn)
    return jnp.where(lanes == ids, one, zero)


def adjacency_kernel(first, last, fresh, final, idle, plan_ref, ready, edge_ref, *refs):
    refs = refs[idle:] if fresh else refs[2 + idle :]
    adj_ref, deg_ref, refs = refs[0], refs[1], refs[2:]
    width = adj_ref.shape[1]
    edges = edge_ref.shape[1]
    if fresh:
        deg_ref[...] = jnp.zeros_like(deg_ref)
    lanes = lax.broadcasted_iota(jnp.int32, (width, edges), 0).astype(jnp.int8)
    ready()

    def body(i, carry):
        base = pl.multiple_of(i * 8, 8)
        both = edge_ref[pl.ds(base, 8), :]
        src, dst = (both & 255).astype(jnp.int8), (both >> 8).astype(jnp.int8)
        for j in range(8):
            spread, collect = one_hot(src[j : j + 1], lanes), one_hot(dst[j : j + 1], lanes)
            adj = lax.dot_general(spread, collect, NT, preferred_element_type=jnp.float32)
            adj_ref[base + j] = adj.astype(jnp.bfloat16)
            deg_ref[plan_ref[ROWS + base + j]] += jnp.sum(adj.reshape(width // 8, 8, width), axis=0)
        return carry

    lax.fori_loop(first, last, body, 0)
    if final:
        inv_ref = refs[0]
        blocks = inv_ref.shape[0]
        degree = jnp.sum(deg_ref[:blocks], axis=1, keepdims=True)
        inv_ref[...] = 1.0 / jnp.maximum(degree, 1.0)


def adjacency(k, plan, edges, blocks, width, state=(), idle=()):
    slots, count = edges.shape
    fresh, final = k == 0, k == len(CUTS) - 2
    outs = [
        jax.ShapeDtypeStruct((slots, width, width), jnp.bfloat16),
        jax.ShapeDtypeStruct((blocks + 1, 8, width), jnp.float32),
    ]
    if final:
        outs.append(jax.ShapeDtypeStruct((blocks, 1, width), jnp.float32))
    return call(
        functools.partial(adjacency_kernel, CUTS[k], CUTS[k + 1], fresh, final, len(idle)),
        outs,
        (edges, *state),
        plan,
        aliases=None if fresh else {2: 0, 3: 1},
        name="adjacency",
        idle=idle,
    )


def copy_all(copies):
    for copy in copies:
        copy.start()
    for copy in copies:
        copy.wait()


def join_kernel(kept_ref, *refs):
    near, mid, (deg_ref, near_ref, mid_ref, *outs), sems = refs[:4], refs[4:7], refs[7:-1], refs[-1]
    rows = mid[0].shape[0]
    half = rows // 2
    copy_all([
        pltpu.make_async_copy(ref, out.at[pl.ds(k * rows, rows)], sems.at[at + k])
        for at, out, pieces in ((0, mid_ref, mid), (3, near_ref, near))
        for k, ref in enumerate(pieces)
    ])
    outs[0][...] = mid_ref[rows : rows + half]
    outs[1][...] = mid_ref[half:rows]


def join(near, mid, kept):
    rows, cols, width = mid[0].shape
    sizes = (4 * rows, 3 * rows) + (rows // 2,) * 2
    return call(
        join_kernel,
        [jax.ShapeDtypeStruct(kept.shape, kept.dtype)]
        + [jax.ShapeDtypeStruct((n, cols, width), jnp.bfloat16) for n in sizes],
        (kept,),
        scratch=[pltpu.SemaphoreType.DMA((7,))],
        aliases={0: 0},
        idle=(*near, *mid),
        name="join",
    )


def far_kernel(one_ref, two_ref, kept_ref, sum_ref, far_ref):
    rows = one_ref.shape[0]
    far_ref[:rows] = one_ref[...]
    far_ref[rows:] = two_ref[...]


def join_far(pieces, sums):
    rows, cols, width = pieces[0].shape
    return call(
        far_kernel,
        [
            jax.ShapeDtypeStruct(sums.shape, sums.dtype),
            jax.ShapeDtypeStruct((2 * rows, cols, width), jnp.bfloat16),
        ],
        (*pieces, sums),
        aliases={2: 0},
        name="join",
    )


def ranged(start, stop, body, unroll=UNROLL):
    def step(i, carry):
        for j in range(unroll):
            spot = start + i * unroll + j
            body(jnp.minimum(spot, stop - 1), spot < stop)
        return carry

    lax.fori_loop(0, (stop - start + unroll - 1) // unroll, step, 0)


def fields(item):
    return item & 127, (item >> 7) & 31, (item >> 12) & 31, (item >> 17) & 15, item >> 21


def mean_kernel(low, high, fresh, final, turns, idle, plan_ref, ready, adj_ref, *refs):
    if fresh:
        weight_ref, here_ref, swap_ref, refs = *refs[:3], refs[3 + idle :]
    else:
        here_ref, swap_ref, refs = *refs[:2], refs[2:]
    if not fresh:
        refs = refs[1:]
    if final:
        inv_ref, refs = refs[0], refs[1:]
    if turns:
        for k in range(2):
            refs[1][k] = weight_ref[k]
            refs[1][2 + k] = weight_ref[k].T
    sum_ref = refs[0]
    blocks = sum_ref.shape[0] - 1
    slots = adj_ref.shape[0]
    if fresh:
        copies = [
            pltpu.make_async_copy(a, b, refs[-1].at[k])
            for k, (a, b) in enumerate(zip((here_ref, swap_ref), refs[-3:-1]))
        ]
        for copy in copies:
            copy.start()
        here_ref, swap_ref = refs[-3:-1]
        sum_ref[...] = jnp.zeros_like(sum_ref)
    if final:
        out_ref = refs[1]
        parts, rows, cols, width = out_ref.shape
    ready()

    for core, feats_ref in enumerate((here_ref, swap_ref)):
        if fresh:
            copies[core].wait()

        def add(spot, valid):
            slot, row, col, key, _ = fields(plan_ref[spot])
            place = (key - low - 8 * core) * blocks + col
            flow = jnp.dot(feats_ref[place], adj_ref[slot], preferred_element_type=jnp.float32)
            sum_ref[jnp.where(valid, row, blocks)] += flow

        ranged(
            plan_ref[slots + low + 8 * core], plan_ref[slots + high + 8 * core], add,
            16 if high - low == 4 else UNROLL,
        )
    if final:
        mean = (sum_ref[:blocks] * inv_ref[...]).astype(jnp.bfloat16)
        out_ref[...] = mean.reshape(parts, rows, cols, width)


def mean_stage(plan, adj, low, high, pieces, before=None, last=(), parts=0, weights=None, idle=()):
    rows, cols, width = pieces[0].shape
    blocks = rows // (high - low)
    fresh, final = before is None, len(last) > 0
    outs = [jax.ShapeDtypeStruct((blocks + 1, cols, width), jnp.float32)]
    if final:
        outs.append(jax.ShapeDtypeStruct((parts, blocks // parts, cols, width), jnp.bfloat16))
    turns = weights is not None
    if turns:
        outs.append(jax.ShapeDtypeStruct((4,) + weights.shape[1:], jnp.bfloat16))
    scratch = []
    if fresh:
        scratch = [pltpu.VMEM(pieces[0].shape, jnp.bfloat16)] * 2 + [pltpu.SemaphoreType.DMA((2,))]
    return call(
        functools.partial(mean_kernel, low, high, fresh, final, turns, len(idle)),
        outs,
        [adj, weights] if fresh else [adj, *pieces, before, *last],
        plan,
        scratch,
        aliases=None if fresh else {4: 0},
        idle=(*pieces, *idle) if fresh else (),
        name="neighbor_mean",
    )


def dense_kernel(plan_ref, ready, in_ref, xc_ref, turn_ref, inv_ref, adj_ref, out_ref, kept_ref, gs_ref, gn_ref):
    parts, rows, cols, width = in_ref.shape
    feats = parts * cols
    ready()
    here = plan_ref[HERE]
    for i in range(rows):
        mean = in_ref[:, i].reshape(feats, width)
        x = xc_ref[:, i].reshape(feats, width)
        cot = xc_ref[:, rows + i].reshape(feats, width).astype(jnp.float32)
        preact = jnp.dot(turn_ref[2], x, preferred_element_type=jnp.float32)
        preact = preact + jnp.dot(turn_ref[3], mean, preferred_element_type=jnp.float32)
        gate = jax.nn.sigmoid(preact)
        hidden = (preact * gate).astype(jnp.bfloat16)
        out_ref[:, rows + i] = hidden.reshape(parts, cols, width)
        out_grad = (cot * gate * (1.0 + preact * (1.0 - gate))).astype(jnp.bfloat16)
        self_term = jnp.dot(turn_ref[0], out_grad, preferred_element_type=jnp.float32)
        out_ref[:, 2 * rows + i] = self_term.astype(jnp.bfloat16).reshape(parts, cols, width)
        pre = jnp.dot(turn_ref[1], out_grad, preferred_element_type=jnp.float32)
        pre = pre * inv_ref[here * rows + i]
        out_ref[:, i] = pre.astype(jnp.bfloat16).reshape(parts, cols, width)
        for ref, left in ((gs_ref, x), (gn_ref, mean)):
            term = lax.dot_general(left, out_grad, NT, preferred_element_type=jnp.float32)
            ref[...] = ref[...] + term if i else term
    for k, ref in enumerate((gs_ref, gn_ref)):
        out_ref[:, 3 * rows + k] = ref[...].astype(jnp.bfloat16).reshape(parts, cols, width)


def dense(plan, packed, x_cot, turn, inverse, adj):
    parts, rows, cols, width = packed.shape
    feats = parts * cols
    grad = pltpu.VMEM((feats, feats), jnp.float32)
    return call(
        dense_kernel,
        [
            jax.ShapeDtypeStruct((parts, 3 * rows + 2, cols, width), jnp.bfloat16),
            jax.ShapeDtypeStruct(adj.shape, adj.dtype),
        ],
        (packed, x_cot, turn, inverse, adj),
        plan,
        [grad, grad],
        aliases={5: 1},
        name="dense",
    )


def back_kernel(
    low, high, adds, takes, cuts, tail, idle, plan_ref, ready, grads_ref, adj_ref, *refs
):
    received, refs = refs[: len(adds)], refs[len(adds) :]
    tails, refs = refs[: len(takes)], refs[len(takes) :]
    outs, sum_ref = refs[idle + 1 :], refs[-1]
    slots = adj_ref.shape[0]
    total = sum_ref.shape[0] - 1
    blocks = total // (high - low)
    sum_ref[...] = jnp.zeros_like(sum_ref)
    for (at, rows, skip), ref in zip(adds, received):
        sum_ref[at : at + rows] += ref[skip : skip + rows].astype(jnp.float32)

    ready()

    def add(spot, valid):
        slot, _, col, key, place = fields(plan_ref[spot])
        back = lax.dot_general(
            grads_ref[place], adj_ref[slot], NT, preferred_element_type=jnp.float32
        )
        spot = jnp.where(valid, (key - (low & 7)) * blocks + col - (low & 8) * blocks, total)
        sum_ref[spot] += back.astype(jnp.bfloat16).astype(jnp.float32)

    ranged(plan_ref[slots + low], plan_ref[slots + high], add)
    at = 0
    for (rows, with_tail), out in zip(cuts, outs):
        out[:rows] = sum_ref[at : at + rows].astype(out.dtype)
        at += rows
    if tail:
        if len(tails) == 1 and not takes[0]:
            chunks = tails[0]
            value = sum(
                chunks[k, -2:].astype(jnp.float32) for k in range(chunks.shape[0])
            )
        else:
            value = sum(
                ref[at : at + 2].astype(jnp.float32) for at, ref in zip(takes, tails)
            )
        value = value.astype(jnp.bfloat16)
        outs[len(cuts)][...] = value
        for (rows, with_tail), out in zip(cuts, outs):
            if with_tail:
                out[rows:] = value


def back_stage(plan, grads, adj, low, high, cuts, received=(), tails=(), idle=(), name=None):
    slots, width, _ = adj.shape
    cols = grads.shape[1]
    blocks = sum(rows for rows, _, _ in cuts) // (high - low)
    shapes = [
        jax.ShapeDtypeStruct((rows + (2 if with_tail else 0), cols, width), dtype)
        for rows, dtype, with_tail in cuts
    ]
    if tails:
        shapes.append(jax.ShapeDtypeStruct((2, cols, width), jnp.bfloat16))
    kept = jax.ShapeDtypeStruct(adj.shape, adj.dtype)
    count = 3 + len(received) + len(tails)
    return call(
        functools.partial(
            back_kernel,
            low,
            high,
            tuple((at, rows, sum(skip)) for at, rows, _, *skip in received),
            tuple(at for at, _ in tails),
            tuple((rows, with_tail) for rows, _, with_tail in cuts),
            len(tails) > 0,
            len(idle),
        ),
        [kept] + shapes + [jax.ShapeDtypeStruct(v.shape, v.dtype) for v in idle],
        (grads, adj, *[entry[2] for entry in received], *[v for _, v in tails]),
        plan,
        [pltpu.VMEM(((high - low) * blocks + 1, cols, width), jnp.float32)],
        aliases={2: 0, **{count + i: 1 + len(shapes) + i for i in range(len(idle))}},
        name=name,
        idle=idle,
        idle_out=len(idle),
    )


def relay_kernel(
    z_more_ref, y_own_ref, y_more_ref, y_less_ref, z_two_ref, own_ref, rest_ref,
    up_ref, over_ref, sum_ref,
):
    rows, cols, width = y_own_ref.shape
    full = jnp.float32
    up = z_more_ref[...] + y_more_ref[...].astype(full)
    up_ref[:rows] = (up + z_two_ref[:rows].astype(full)).astype(jnp.bfloat16)
    up_ref[rows:] = z_two_ref[rows:]
    over_ref[...] = (y_own_ref[...] + y_less_ref[:rows].astype(full)).astype(jnp.bfloat16)
    per = rows // rest_ref.shape[0]
    term = rest_ref[:, 2 * per : 3 * per].reshape(rows, cols, width).astype(full)
    sum_ref[...] = own_ref[...] + term


def relay(*values):
    rows, cols, width = values[0].shape
    sizes = ((rows + 2, jnp.bfloat16), (rows, jnp.bfloat16), (rows, jnp.float32))
    shapes = [jax.ShapeDtypeStruct((n, cols, width), dtype) for n, dtype in sizes]
    return call(relay_kernel, shapes, values, name="relay")


def finish_kernel(
    scale, own_ref, less_ref, more_ref, over_ref, g_ref, down_ref, up_ref, input_ref, gs_ref, gn_ref
):
    blocks = own_ref.shape[0]
    full = jnp.float32
    back = own_ref[...] + less_ref[...].astype(full)
    back = back + more_ref[:blocks].astype(full) + over_ref[...].astype(full)
    input_ref[...] = back.astype(jnp.bfloat16)
    total = g_ref[...].astype(full) + more_ref[blocks:].astype(full)
    total = total + (down_ref[blocks:].astype(full) + up_ref[blocks:].astype(full))
    total = total * scale
    gs_ref[...] = total[0]
    gn_ref[...] = total[1]


def finish(scale, *values):
    blocks, cols, width = values[0].shape
    moved = jax.ShapeDtypeStruct((blocks, cols, width), jnp.bfloat16)
    grad = jax.ShapeDtypeStruct((cols, width), jnp.float32)
    return call(
        functools.partial(finish_kernel, scale), [moved, grad, grad], values, name="finish"
    )


def make_plan(tile_row, tile_owner, tile_col, tile_count, blocks):
    slots = tile_row.shape[0]
    ids = jnp.arange(slots, dtype=jnp.int32)
    me = lax.axis_index("blk").astype(jnp.int32)
    owner = tile_owner[:, 0]
    code = ((owner ^ me) >> 3) * 4 + (((owner >> 1) - (me >> 1)) & 3)
    view = sum(jnp.where(code == k, VIEW[k], 0) for k in range(8))
    key = view + 8 * ((owner ^ me) & 1)
    key = jnp.where(ids < tile_count[0], key, 16)
    moved = tile_row + 8 * (tile_row // 3)
    item = ids + (tile_row << 7) + (tile_col << 12) + ((key & 15) << 17) + (moved << 21)
    full = key * slots + ids
    rank = jnp.sum((full[None, :] < full[:, None]).astype(jnp.int32), axis=1)
    ordered = jnp.sum(jnp.where(rank[None, :] == ids[:, None], item[None, :], 0), axis=1)
    starts = jnp.sum((key[None, :] < jnp.arange(32, dtype=jnp.int32)[:, None]).astype(jnp.int32), axis=1)
    here = jnp.full((8,), lax.axis_index("col"), jnp.int32)
    rows = jnp.where(ids < tile_count[0], tile_row, blocks)
    return jnp.concatenate([ordered, starts, here, rows])


def local(
    features, cotangent, w_self, w_neigh, tile_row, tile_owner, tile_col, tile_count,
    edge_dst, edge_src,
):
    blocks, cols, width = features.shape
    n_blk, n_col = lax.axis_size("blk"), lax.axis_size("col")
    per = blocks // n_col
    third = blocks // 3

    def over_col(a, rows):
        moved = lax.all_to_all(a.reshape(n_col, rows * cols, width), "col", 0, 0)
        return moved.reshape(n_col, rows, cols, width)

    own = features
    z_less, z_more, y_own = send(own, "up"), send(own, "down"), send(own, "over")
    plan = make_plan(tile_row, tile_owner, tile_col, tile_count, blocks)
    build = functools.partial(
        adjacency, plan=plan, edges=edge_src + (edge_dst << 8), blocks=blocks, width=width
    )
    x_cot = over_col(
        jnp.concatenate([a.reshape(n_col, per, cols, width) for a in (features, cotangent)], axis=1),
        2 * per,
    )
    y_more, y_less, z_two = send(z_more, "over"), send(y_own, "up"), send(z_more, "down")
    adj, deg = build(0, idle=(x_cot,))
    deg, near, mid, *cut = join((own, z_less, z_more, y_own), (y_more, y_less, z_two), deg)
    near_swap = send(near, "core")
    cut = [send(cut[0], "up"), send(cut[1], "down")]
    mid_swap = send(mid, "core")
    adj, deg, inverse = build(1, state=(adj, deg))
    sums, turn = mean_stage(
        plan, adj, 0, 4, [near, near_swap], weights=jnp.stack([w_self, w_neigh]), idle=(mid,)
    )
    sums, y_two = join_far(cut, sums)
    y_swap = send(y_two, "core")
    (sums,) = mean_stage(plan, adj, 4, 7, [mid, mid_swap], sums)
    _, packed = mean_stage(
        plan, adj, 7, 8, [y_two, y_swap], sums, (inverse,), n_col
    )

    out, adj = dense(plan, over_col(packed, per), x_cot, turn, inverse, adj)
    moved = over_col(out, 3 * per + 2)
    hidden = moved[:, per : 2 * per].reshape(blocks, cols, width)
    grads = moved.reshape(n_col * (3 * per + 2), cols, width)

    half, full = jnp.bfloat16, jnp.float32
    back = functools.partial(back_stage, plan, grads)
    adj, far, g = back(adj, 15, 16, name="sums_far_swap", cuts=[(blocks, half, True)], tails=[(0, moved)])
    far = send(far, "core")
    adj, mid = back(adj, 12, 15, name="sums_mid_swap", cuts=[(3 * blocks, half, False)])
    adj, *cut, g, mid = back(
        adj, 7, 8, name="sums_far_own", cuts=[(third, half, True), (third, half, False), (third, half, False)],
        received=[(0, blocks, far)], tails=[(0, g), (blocks, far)], idle=(mid,),
    )
    mid = send(mid, "core")
    cut = [send(cut[0], "over"), send(cut[1], "down"), send(cut[2], "up")]
    adj, near = back(adj, 8, 12, name="sums_near_swap", cuts=[(4 * blocks, half, False)])
    adj, y_more, y_less, z_two, g, near = back(
        adj, 4, 7, name="sums_mid_own", cuts=[(blocks, half, False), (blocks, half, True), (blocks, half, True)],
        received=[(0, 3 * blocks, mid), (2 * blocks, third, cut[0]), (blocks + third, third, cut[1]),
         (2 * third, third, cut[2])],
        tails=[(0, g), (third, cut[0])], idle=(near,),
    )
    near = send(near, "core")
    y_more, y_less, z_two = send(y_more, "over"), send(y_less, "down"), send(z_two, "up")
    adj, own, z_less, z_more, y_own = back(
        adj, 0, 4, name="sums_near_own", cuts=
        [(blocks, full, False), (blocks, half, False), (blocks, full, False), (blocks, full, False)],
        received=[(0, 4 * blocks, near)],
    )
    z_less = send(z_less, "down")
    z_more, y_own, own = relay(z_more, y_own, y_more, y_less, z_two, own, moved)
    z_more, y_own = send(z_more, "up"), send(y_own, "over")
    scale = 1.0 / math.sqrt(blocks * width * n_blk)
    return (hidden, *finish(scale, own, z_less, z_more, y_own, g, y_less, z_two))


def solution(mesh):
    placed = (
        P("blk", "col", None),
        P("blk", "col", None),
        P(),
        P(),
        P("blk"),
        P("blk", None),
        P("blk"),
        P("blk"),
        P("blk", None),
        P("blk", None),
    )
    return jax.shard_map(
        local,
        mesh=mesh,
        in_specs=placed,
        out_specs=(P("blk", "col", None), P("blk", "col", None), P("col", None), P("col", None)),
        check_vma=False,
    )
```

```python
import functools
import math

import jax
import jax.numpy as jnp
from jax import lax
from jax.experimental import pallas as pl
from jax.experimental.pallas import tpu as pltpu
from jax.sharding import PartitionSpec as P

UNROLL = 12
HERE = 160
ROWS = 168
CUTS = (0, 12, 16)
VMEM_BYTES = 14 * 1024 * 1024
NT = (((1,), (1,)), ((), ()))
WHOLE = pl.BlockSpec(memory_space=pltpu.VMEM)
IDLE = pl.BlockSpec(memory_space=pl.ANY)

VIEW = (0, 2, 6, 1, 3, 4, 7, 5)


def turned(i, dz):
    y, z, core = i >> 3, (i >> 1) & 3, i & 1
    return (y << 3) | (((z + dz) % 4) << 1) | core


ROUTES = {
    "up": [(i, turned(i, 1)) for i in range(16)],
    "down": [(i, turned(i, -1)) for i in range(16)],
    "over": [(i, i ^ 8) for i in range(16)],
    "core": [(i, i ^ 1) for i in range(16)],
}


def send(value, route):
    return lax.ppermute(value, "blk", ROUTES[route])


def with_plan(kernel, plan_ref, *refs):
    *refs, held_ref, sem = refs
    copy = pltpu.make_async_copy(plan_ref, held_ref, sem)
    copy.start()
    kernel(held_ref, copy.wait, *refs)


def call(
    kernel, out_shape, operands, plan=None, scratch=(), aliases=None, name=None, idle=(), idle_out=0
):
    scratch = list(scratch)
    if plan is not None:
        kernel = functools.partial(with_plan, kernel)
        scratch += [pltpu.SMEM(plan.shape, plan.dtype), pltpu.SemaphoreType.DMA]
    lead = [] if plan is None else [plan]
    return pl.pallas_call(
        kernel,
        in_specs=[IDLE] * len(lead) + [WHOLE] * len(operands) + [IDLE] * len(idle),
        out_specs=[WHOLE] * (len(out_shape) - idle_out) + [IDLE] * idle_out,
        out_shape=out_shape,
        scratch_shapes=scratch,
        input_output_aliases=aliases or {},
        compiler_params=pltpu.CompilerParams(vmem_limit_bytes=VMEM_BYTES),
        name=name,
    )(*lead, *operands, *idle)


def one_hot(ids, lanes):
    one, zero = jnp.ones((), jnp.float8_e4m3fn), jnp.zeros((), jnp.float8_e4m3fn)
    return jnp.where(lanes == ids, one, zero)


def adjacency_kernel(first, last, fresh, final, idle, plan_ref, ready, edge_ref, *refs):
    refs = refs[idle:] if fresh else refs[2 + idle :]
    adj_ref, deg_ref, refs = refs[0], refs[1], refs[2:]
    width = adj_ref.shape[1]
    edges = edge_ref.shape[1]
    if fresh:
        deg_ref[...] = jnp.zeros_like(deg_ref)
    lanes = lax.broadcasted_iota(jnp.int32, (width, edges), 0).astype(jnp.int8)
    ready()

    def body(i, carry):
        base = pl.multiple_of(i * 8, 8)
        both = edge_ref[pl.ds(base, 8), :]
        src, dst = (both & 255).astype(jnp.int8), (both >> 8).astype(jnp.int8)
        for j in range(8):
            spread, collect = one_hot(src[j : j + 1], lanes), one_hot(dst[j : j + 1], lanes)
            adj = lax.dot_general(spread, collect, NT, preferred_element_type=jnp.float32)
            adj_ref[base + j] = adj.astype(jnp.bfloat16)
            deg_ref[plan_ref[ROWS + base + j]] += jnp.sum(adj.reshape(width // 8, 8, width), axis=0)
        return carry

    lax.fori_loop(first, last, body, 0)
    if final:
        inv_ref = refs[0]
        blocks = inv_ref.shape[0]
        degree = jnp.sum(deg_ref[:blocks], axis=1, keepdims=True)
        inv_ref[...] = 1.0 / jnp.maximum(degree, 1.0)


def adjacency(k, plan, edges, blocks, width, state=(), idle=()):
    slots, count = edges.shape
    fresh, final = k == 0, k == len(CUTS) - 2
    outs = [
        jax.ShapeDtypeStruct((slots, width, width), jnp.bfloat16),
        jax.ShapeDtypeStruct((blocks + 1, 8, width), jnp.float32),
    ]
    if final:
        outs.append(jax.ShapeDtypeStruct((blocks, 1, width), jnp.float32))
    return call(
        functools.partial(adjacency_kernel, CUTS[k], CUTS[k + 1], fresh, final, len(idle)),
        outs,
        (edges, *state),
        plan,
        aliases=None if fresh else {2: 0, 3: 1},
        name="adjacency",
        idle=idle,
    )


def copy_all(copies):
    for copy in copies:
        copy.start()
    for copy in copies:
        copy.wait()


def join_kernel(kept_ref, *refs):
    near, mid, (deg_ref, near_ref, mid_ref, *outs), sems = refs[:4], refs[4:7], refs[7:-1], refs[-1]
    rows = mid[0].shape[0]
    half = rows // 2
    copy_all([
        pltpu.make_async_copy(ref, out.at[pl.ds(k * rows, rows)], sems.at[at + k])
        for at, out, pieces in ((0, mid_ref, mid), (3, near_ref, near))
        for k, ref in enumerate(pieces)
    ])
    outs[0][...] = mid_ref[rows : rows + half]
    outs[1][...] = mid_ref[half:rows]


def join(near, mid, kept):
    rows, cols, width = mid[0].shape
    sizes = (4 * rows, 3 * rows) + (rows // 2,) * 2
    return call(
        join_kernel,
        [jax.ShapeDtypeStruct(kept.shape, kept.dtype)]
        + [jax.ShapeDtypeStruct((n, cols, width), jnp.bfloat16) for n in sizes],
        (kept,),
        scratch=[pltpu.SemaphoreType.DMA((7,))],
        aliases={0: 0},
        idle=(*near, *mid),
        name="join",
    )


def far_kernel(one_ref, two_ref, kept_ref, sum_ref, far_ref):
    rows = one_ref.shape[0]
    far_ref[:rows] = one_ref[...]
    far_ref[rows:] = two_ref[...]


def join_far(pieces, sums):
    rows, cols, width = pieces[0].shape
    return call(
        far_kernel,
        [
            jax.ShapeDtypeStruct(sums.shape, sums.dtype),
            jax.ShapeDtypeStruct((2 * rows, cols, width), jnp.bfloat16),
        ],
        (*pieces, sums),
        aliases={2: 0},
        name="join",
    )


def ranged(start, stop, body, unroll=UNROLL):
    def step(i, carry):
        for j in range(unroll):
            spot = start + i * unroll + j
            body(jnp.minimum(spot, stop - 1), spot < stop)
        return carry

    lax.fori_loop(0, (stop - start + unroll - 1) // unroll, step, 0)


def fields(item):
    return item & 127, (item >> 7) & 31, (item >> 12) & 31, (item >> 17) & 15, item >> 21


def mean_kernel(low, high, fresh, final, turns, idle, plan_ref, ready, adj_ref, *refs):
    if fresh:
        weight_ref, here_ref, swap_ref, refs = *refs[:3], refs[3 + idle :]
    else:
        here_ref, swap_ref, refs = *refs[:2], refs[2:]
    if not fresh:
        refs = refs[1:]
    if final:
        inv_ref, refs = refs[0], refs[1:]
    if turns:
        for k in range(2):
            refs[1][k] = weight_ref[k]
            refs[1][2 + k] = weight_ref[k].T
    sum_ref = refs[0]
    blocks = sum_ref.shape[0] - 1
    slots = adj_ref.shape[0]
    if fresh:
        copies = [
            pltpu.make_async_copy(a, b, refs[-1].at[k])
            for k, (a, b) in enumerate(zip((here_ref, swap_ref), refs[-3:-1]))
        ]
        for copy in copies:
            copy.start()
        here_ref, swap_ref = refs[-3:-1]
        sum_ref[...] = jnp.zeros_like(sum_ref)
    if final:
        out_ref = refs[1]
        parts, rows, cols, width = out_ref.shape
    ready()

    for core, feats_ref in enumerate((here_ref, swap_ref)):
        if fresh:
            copies[core].wait()

        def add(spot, valid):
            slot, row, col, key, _ = fields(plan_ref[spot])
            place = (key - low - 8 * core) * blocks + col
            flow = jnp.dot(feats_ref[place], adj_ref[slot], preferred_element_type=jnp.float32)
            sum_ref[jnp.where(valid, row, blocks)] += flow

        ranged(
            plan_ref[slots + low + 8 * core], plan_ref[slots + high + 8 * core], add,
            UNROLL,
        )
    if final:
        mean = (sum_ref[:blocks] * inv_ref[...]).astype(jnp.bfloat16)
        out_ref[...] = mean.reshape(parts, rows, cols, width)


def mean_stage(plan, adj, low, high, pieces, before=None, last=(), parts=0, weights=None, idle=()):
    rows, cols, width = pieces[0].shape
    blocks = rows // (high - low)
    fresh, final = before is None, len(last) > 0
    outs = [jax.ShapeDtypeStruct((blocks + 1, cols, width), jnp.float32)]
    if final:
        outs.append(jax.ShapeDtypeStruct((parts, blocks // parts, cols, width), jnp.bfloat16))
    turns = weights is not None
    if turns:
        outs.append(jax.ShapeDtypeStruct((4,) + weights.shape[1:], jnp.bfloat16))
    scratch = []
    if fresh:
        scratch = [pltpu.VMEM(pieces[0].shape, jnp.bfloat16)] * 2 + [pltpu.SemaphoreType.DMA((2,))]
    return call(
        functools.partial(mean_kernel, low, high, fresh, final, turns, len(idle)),
        outs,
        [adj, weights] if fresh else [adj, *pieces, before, *last],
        plan,
        scratch,
        aliases=None if fresh else {4: 0},
        idle=(*pieces, *idle) if fresh else (),
        name="neighbor_mean",
    )


def dense_kernel(plan_ref, ready, in_ref, xc_ref, turn_ref, inv_ref, adj_ref, out_ref, kept_ref, gs_ref, gn_ref):
    parts, rows, cols, width = in_ref.shape
    feats = parts * cols
    ready()
    here = plan_ref[HERE]
    for i in range(rows):
        mean = in_ref[:, i].reshape(feats, width)
        x = xc_ref[:, i].reshape(feats, width)
        cot = xc_ref[:, rows + i].reshape(feats, width).astype(jnp.float32)
        preact = jnp.dot(turn_ref[2], x, preferred_element_type=jnp.float32)
        preact = preact + jnp.dot(turn_ref[3], mean, preferred_element_type=jnp.float32)
        gate = jax.nn.sigmoid(preact)
        hidden = (preact * gate).astype(jnp.bfloat16)
        out_ref[:, rows + i] = hidden.reshape(parts, cols, width)
        out_grad = (cot * gate * (1.0 + preact * (1.0 - gate))).astype(jnp.bfloat16)
        self_term = jnp.dot(turn_ref[0], out_grad, preferred_element_type=jnp.float32)
        out_ref[:, 2 * rows + i] = self_term.astype(jnp.bfloat16).reshape(parts, cols, width)
        pre = jnp.dot(turn_ref[1], out_grad, preferred_element_type=jnp.float32)
        pre = pre * inv_ref[here * rows + i]
        out_ref[:, i] = pre.astype(jnp.bfloat16).reshape(parts, cols, width)
        for ref, left in ((gs_ref, x), (gn_ref, mean)):
            term = lax.dot_general(left, out_grad, NT, preferred_element_type=jnp.float32)
            ref[...] = ref[...] + term if i else term
    for k, ref in enumerate((gs_ref, gn_ref)):
        out_ref[:, 3 * rows + k] = ref[...].astype(jnp.bfloat16).reshape(parts, cols, width)


def dense(plan, packed, x_cot, turn, inverse, adj):
    parts, rows, cols, width = packed.shape
    feats = parts * cols
    grad = pltpu.VMEM((feats, feats), jnp.float32)
    return call(
        dense_kernel,
        [
            jax.ShapeDtypeStruct((parts, 3 * rows + 2, cols, width), jnp.bfloat16),
            jax.ShapeDtypeStruct(adj.shape, adj.dtype),
        ],
        (packed, x_cot, turn, inverse, adj),
        plan,
        [grad, grad],
        aliases={5: 1},
        name="dense",
    )


def back_kernel(
    low, high, adds, takes, cuts, tail, idle, plan_ref, ready, grads_ref, adj_ref, *refs
):
    received, refs = refs[: len(adds)], refs[len(adds) :]
    tails, refs = refs[: len(takes)], refs[len(takes) :]
    outs, sum_ref = refs[idle + 1 :], refs[-1]
    slots = adj_ref.shape[0]
    total = sum_ref.shape[0] - 1
    blocks = total // (high - low)
    sum_ref[...] = jnp.zeros_like(sum_ref)
    for (at, rows, skip), ref in zip(adds, received):
        sum_ref[at : at + rows] += ref[skip : skip + rows].astype(jnp.float32)

    ready()

    def add(spot, valid):
        slot, _, col, key, place = fields(plan_ref[spot])
        back = lax.dot_general(
            grads_ref[place], adj_ref[slot], NT, preferred_element_type=jnp.float32
        )
        spot = jnp.where(valid, (key - (low & 7)) * blocks + col - (low & 8) * blocks, total)
        sum_ref[spot] += back.astype(jnp.bfloat16).astype(jnp.float32)

    ranged(plan_ref[slots + low], plan_ref[slots + high], add)
    at = 0
    for (rows, with_tail), out in zip(cuts, outs):
        out[:rows] = sum_ref[at : at + rows].astype(out.dtype)
        at += rows
    if tail:
        if len(tails) == 1 and not takes[0]:
            chunks = tails[0]
            value = sum(
                chunks[k, -2:].astype(jnp.float32) for k in range(chunks.shape[0])
            )
        else:
            value = sum(
                ref[at : at + 2].astype(jnp.float32) for at, ref in zip(takes, tails)
            )
        value = value.astype(jnp.bfloat16)
        outs[len(cuts)][...] = value
        for (rows, with_tail), out in zip(cuts, outs):
            if with_tail:
                out[rows:] = value


def back_stage(plan, grads, adj, low, high, cuts, received=(), tails=(), idle=(), name=None):
    slots, width, _ = adj.shape
    cols = grads.shape[1]
    blocks = sum(rows for rows, _, _ in cuts) // (high - low)
    shapes = [
        jax.ShapeDtypeStruct((rows + (2 if with_tail else 0), cols, width), dtype)
        for rows, dtype, with_tail in cuts
    ]
    if tails:
        shapes.append(jax.ShapeDtypeStruct((2, cols, width), jnp.bfloat16))
    kept = jax.ShapeDtypeStruct(adj.shape, adj.dtype)
    count = 3 + len(received) + len(tails)
    return call(
        functools.partial(
            back_kernel,
            low,
            high,
            tuple((at, rows, sum(skip)) for at, rows, _, *skip in received),
            tuple(at for at, _ in tails),
            tuple((rows, with_tail) for rows, _, with_tail in cuts),
            len(tails) > 0,
            len(idle),
        ),
        [kept] + shapes + [jax.ShapeDtypeStruct(v.shape, v.dtype) for v in idle],
        (grads, adj, *[entry[2] for entry in received], *[v for _, v in tails]),
        plan,
        [pltpu.VMEM(((high - low) * blocks + 1, cols, width), jnp.float32)],
        aliases={2: 0, **{count + i: 1 + len(shapes) + i for i in range(len(idle))}},
        name=name,
        idle=idle,
        idle_out=len(idle),
    )


def relay_kernel(
    z_more_ref, y_own_ref, y_more_ref, y_less_ref, z_two_ref, own_ref, rest_ref,
    up_ref, over_ref, sum_ref,
):
    rows, cols, width = y_own_ref.shape
    full = jnp.float32
    up = z_more_ref[...] + y_more_ref[...].astype(full)
    up_ref[:rows] = (up + z_two_ref[:rows].astype(full)).astype(jnp.bfloat16)
    up_ref[rows:] = z_two_ref[rows:]
    over_ref[...] = (y_own_ref[...] + y_less_ref[:rows].astype(full)).astype(jnp.bfloat16)
    per = rows // rest_ref.shape[0]
    term = rest_ref[:, 2 * per : 3 * per].reshape(rows, cols, width).astype(full)
    sum_ref[...] = own_ref[...] + term


def relay(*values):
    rows, cols, width = values[0].shape
    sizes = ((rows + 2, jnp.bfloat16), (rows, jnp.bfloat16), (rows, jnp.float32))
    shapes = [jax.ShapeDtypeStruct((n, cols, width), dtype) for n, dtype in sizes]
    return call(relay_kernel, shapes, values, name="relay")


def finish_kernel(
    scale, own_ref, less_ref, more_ref, over_ref, g_ref, down_ref, up_ref, input_ref, gs_ref, gn_ref
):
    blocks = own_ref.shape[0]
    full = jnp.float32
    back = own_ref[...] + less_ref[...].astype(full)
    back = back + more_ref[:blocks].astype(full) + over_ref[...].astype(full)
    input_ref[...] = back.astype(jnp.bfloat16)
    total = g_ref[...].astype(full) + more_ref[blocks:].astype(full)
    total = total + (down_ref[blocks:].astype(full) + up_ref[blocks:].astype(full))
    total = total * scale
    gs_ref[...] = total[0]
    gn_ref[...] = total[1]


def finish(scale, *values):
    blocks, cols, width = values[0].shape
    moved = jax.ShapeDtypeStruct((blocks, cols, width), jnp.bfloat16)
    grad = jax.ShapeDtypeStruct((cols, width), jnp.float32)
    return call(
        functools.partial(finish_kernel, scale), [moved, grad, grad], values, name="finish"
    )


def make_plan(tile_row, tile_owner, tile_col, tile_count, blocks):
    slots = tile_row.shape[0]
    ids = jnp.arange(slots, dtype=jnp.int32)
    me = lax.axis_index("blk").astype(jnp.int32)
    owner = tile_owner[:, 0]
    code = ((owner ^ me) >> 3) * 4 + (((owner >> 1) - (me >> 1)) & 3)
    view = sum(jnp.where(code == k, VIEW[k], 0) for k in range(8))
    key = view + 8 * ((owner ^ me) & 1)
    key = jnp.where(ids < tile_count[0], key, 16)
    moved = tile_row + 8 * (tile_row // 3)
    item = ids + (tile_row << 7) + (tile_col << 12) + ((key & 15) << 17) + (moved << 21)
    full = key * slots + ids
    rank = jnp.sum((full[None, :] < full[:, None]).astype(jnp.int32), axis=1)
    ordered = jnp.sum(jnp.where(rank[None, :] == ids[:, None], item[None, :], 0), axis=1)
    starts = jnp.sum((key[None, :] < jnp.arange(32, dtype=jnp.int32)[:, None]).astype(jnp.int32), axis=1)
    here = jnp.full((8,), lax.axis_index("col"), jnp.int32)
    rows = jnp.where(ids < tile_count[0], tile_row, blocks)
    return jnp.concatenate([ordered, starts, here, rows])


def local(
    features, cotangent, w_self, w_neigh, tile_row, tile_owner, tile_col, tile_count,
    edge_dst, edge_src,
):
    blocks, cols, width = features.shape
    n_blk, n_col = lax.axis_size("blk"), lax.axis_size("col")
    per = blocks // n_col
    third = blocks // 3

    def over_col(a, rows):
        moved = lax.all_to_all(a.reshape(n_col, rows * cols, width), "col", 0, 0)
        return moved.reshape(n_col, rows, cols, width)

    own = features
    z_less, z_more, y_own = send(own, "up"), send(own, "down"), send(own, "over")
    plan = make_plan(tile_row, tile_owner, tile_col, tile_count, blocks)
    build = functools.partial(
        adjacency, plan=plan, edges=edge_src + (edge_dst << 8), blocks=blocks, width=width
    )
    x_cot = over_col(
        jnp.concatenate([a.reshape(n_col, per, cols, width) for a in (features, cotangent)], axis=1),
        2 * per,
    )
    y_more, y_less, z_two = send(z_more, "over"), send(y_own, "up"), send(z_more, "down")
    adj, deg = build(0, idle=(x_cot,))
    deg, near, mid, *cut = join((own, z_less, z_more, y_own), (y_more, y_less, z_two), deg)
    near_swap = send(near, "core")
    cut = [send(cut[0], "up"), send(cut[1], "down")]
    mid_swap = send(mid, "core")
    adj, deg, inverse = build(1, state=(adj, deg))
    sums, turn = mean_stage(
        plan, adj, 0, 4, [near, near_swap], weights=jnp.stack([w_self, w_neigh]), idle=(mid,)
    )
    sums, y_two = join_far(cut, sums)
    y_swap = send(y_two, "core")
    (sums,) = mean_stage(plan, adj, 4, 7, [mid, mid_swap], sums)
    _, packed = mean_stage(
        plan, adj, 7, 8, [y_two, y_swap], sums, (inverse,), n_col
    )

    out, adj = dense(plan, over_col(packed, per), x_cot, turn, inverse, adj)
    moved = over_col(out, 3 * per + 2)
    hidden = moved[:, per : 2 * per].reshape(blocks, cols, width)
    grads = moved.reshape(n_col * (3 * per + 2), cols, width)

    half, full = jnp.bfloat16, jnp.float32
    back = functools.partial(back_stage, plan, grads)
    adj, far, g = back(adj, 15, 16, name="sums_far_swap", cuts=[(blocks, half, True)], tails=[(0, moved)])
    far = send(far, "core")
    adj, mid = back(adj, 12, 15, name="sums_mid_swap", cuts=[(3 * blocks, half, False)])
    adj, *cut, g, mid = back(
        adj, 7, 8, name="sums_far_own", cuts=[(third, half, True), (third, half, False), (third, half, False)],
        received=[(0, blocks, far)], tails=[(0, g), (blocks, far)], idle=(mid,),
    )
    mid = send(mid, "core")
    cut = [send(cut[0], "over"), send(cut[1], "down"), send(cut[2], "up")]
    adj, near = back(adj, 8, 12, name="sums_near_swap", cuts=[(4 * blocks, half, False)])
    adj, y_more, y_less, z_two, g, near = back(
        adj, 4, 7, name="sums_mid_own", cuts=[(blocks, half, False), (blocks, half, True), (blocks, half, True)],
        received=[(0, 3 * blocks, mid), (2 * blocks, third, cut[0]), (blocks + third, third, cut[1]),
         (2 * third, third, cut[2])],
        tails=[(0, g), (third, cut[0])], idle=(near,),
    )
    near = send(near, "core")
    y_more, y_less, z_two = send(y_more, "over"), send(y_less, "down"), send(z_two, "up")
    adj, own, z_less, z_more, y_own = back(
        adj, 0, 4, name="sums_near_own", cuts=
        [(blocks, full, False), (blocks, half, False), (blocks, full, False), (blocks, full, False)],
        received=[(0, 4 * blocks, near)],
    )
    z_less = send(z_less, "down")
    z_more, y_own, own = relay(z_more, y_own, y_more, y_less, z_two, own, moved)
    z_more, y_own = send(z_more, "up"), send(y_own, "over")
    scale = 1.0 / math.sqrt(blocks * width * n_blk)
    return (hidden, *finish(scale, own, z_less, z_more, y_own, g, y_less, z_two))


def solution(mesh):
    placed = (
        P("blk", "col", None),
        P("blk", "col", None),
        P(),
        P(),
        P("blk"),
        P("blk", None),
        P("blk"),
        P("blk"),
        P("blk", None),
        P("blk", None),
    )
    return jax.shard_map(
        local,
        mesh=mesh,
        in_specs=placed,
        out_specs=(P("blk", "col", None), P("blk", "col", None), P("col", None), P("col", None)),
        check_vma=False,
    )
```
